32 devices in a mesh: dp: 8 (over z, core), frame: 4 (over y, x).
Axes of the slice: x: 2, y: 2, z: 4, core: 2. Of those that a mesh axis runs over, the one named last changes fastest.
Arguments:
- latents: bfloat16 [8, 8, 128, 1280], P('dp', 'frame'), may hold values from -330 to 330
- timestep: int32 [8], P('dp'), may hold values from 0 to 999
- norm_gain: float32 [1280], replicated, may hold values from 0.1 to 1.9
- time_weight: bfloat16 [320, 1280], P('dp'), may hold values from -0.3125 to 0.3125
- conv_weight: bfloat16 [3, 1280, 1280], P(None, ('dp', 'frame')), may hold values from -0.09375 to 0.09375
- attend_weight: bfloat16 [1280, 3840], P(('dp', 'frame')), may hold values from -0.3354102 to 0.3354102
- output_weight: bfloat16 [1280, 1280], P(('dp', 'frame')), may hold values from -0.15625 to 0.15625
Outputs:
- block_out: bfloat16 [8, 8, 128, 1280], P('dp', 'frame')
The draws below stay inside these ranges and needn't reach their ends.
All inputs are finite; a program needn't handle non-finite values.
Results may differ from the reference program's by a relative error of at most 0.0051.
Values may be sent and summed in bfloat16 or wider, within the bound.
A program may use at most 128 MiB of HBM per device.

```python
import math
import jax
import jax.numpy as jnp
from jax import lax

C = 1280
HEADS = 20
HD = 64
GROUPS = 32
TEMB = 320
PIX = 128
FRAMES = 8
CLIPS = 8


def draw_latents(key, part):
    key_base, key_pixel, key_chan, key_frame = jax.random.split(key, 4)
    shape = (CLIPS, FRAMES, PIX, C)
    ladder = jnp.arange(FRAMES, dtype=jnp.float32)
    frame_ladder = 3.0 ** (ladder / max(FRAMES - 1, 1))
    frame_factor = jnp.exp(jax.random.uniform(key_frame, (CLIPS, FRAMES, 1, 1), jnp.float32, math.log(0.5), math.log(2.0)))
    frame_scale = frame_ladder[None, :, None, None] * frame_factor
    pixel_scale = jnp.exp(jax.random.uniform(key_pixel, (CLIPS, 1, PIX, 1), jnp.float32, math.log(0.3), math.log(3.0)))
    chan_scale = jnp.exp(jax.random.uniform(key_chan, (1, 1, 1, C), jnp.float32, math.log(0.3), math.log(3.0)))
    base = jnp.clip(jax.random.normal(key_base, shape, jnp.float32), -6.0, 6.0)
    values = base * frame_scale * pixel_scale * chan_scale
    return values.astype(jnp.bfloat16)


def draw_attend_weight(key, part):
    key_query = jax.random.fold_in(key, 0)
    scale = 1.0 / math.sqrt(C)
    values = jnp.clip(jax.random.normal(key_query, (C, 3 * C), jnp.float32), -6.0, 6.0) * scale
    return values.astype(jnp.bfloat16)


def place_ends(array, stream_key, low, largest):
    longest = array.shape.index(max(array.shape))
    spots = []
    for shift in (0, 1):
        where = [jax.random.randint(jax.random.fold_in(stream_key, axis), (), 0, length) for axis, length in enumerate(array.shape)]
        where[longest] = (where[longest] + shift) % array.shape[longest]
        spots.append(tuple(where))
    return array.at[spots[0]].set(low).at[spots[1]].set(largest)


def block_levels(key, extent, cuts, least, top_value):
    def one(dim, blocks):
        heights = jax.random.uniform(jax.random.fold_in(jax.random.fold_in(key, 6), dim), (blocks,), jnp.float32, least / len(cuts), top_value / len(cuts))
        return jnp.repeat(jnp.exp(heights), extent[dim] // blocks).reshape((-1,) + (1,) * (len(extent) - dim - 1))

    gain = one(*cuts[0])
    for cut in cuts[1:]:
        gain = gain * one(*cut)
    return gain


def scatter_about(rng, extent, width, limit, cuts=(), held_as=jnp.bfloat16):
    entries = jax.random.normal(rng, extent, jnp.float32) * width
    if len(cuts) > 0:
        entries = block_levels(rng, extent, cuts, -0.22, 0.18) * entries
    return jnp.clip(entries, min=-limit, max=limit).astype(held_as)


def setup_inputs(seed: int = 0) -> dict:
    key_of = jax.random.split(jax.random.key(seed), 8)
    return {
        "latents": draw_latents(jax.random.fold_in(key_of[7], 71), 0),
        "timestep": place_ends(jax.random.randint(key_of[1], (CLIPS,), 0, 1000), jax.random.fold_in(key_of[1], 1), 0, 999).astype(jnp.int32),
        "norm_gain": jnp.clip(1.0 + 0.18 * jax.random.normal(key_of[2], (C,), jnp.float32), 0.1, 1.9),
        "time_weight": scatter_about(key_of[3], (TEMB, C), TEMB ** -0.5, 0.3125, ((0, 8),)),
        "conv_weight": scatter_about(key_of[4], (3, C, C), (3 * C) ** -0.5, 0.09375, ((1, 32),)),
        "attend_weight": draw_attend_weight(jax.random.fold_in(key_of[7], 71), 0),
        "output_weight": scatter_about(key_of[6], (C, C), C ** -0.5, 0.15625, ((0, 32),)),
    }


def sinusoid(timestep):
    half_dim = TEMB // 2
    ladder = jnp.arange(half_dim, dtype=jnp.float32)
    freqs = jnp.exp(-math.log(10000.0) * ladder / half_dim)
    angles = timestep.astype(jnp.float32)[:, None] * freqs[None, :]
    return jnp.concatenate([jnp.cos(angles), jnp.sin(angles)], axis=-1)

def reference(latents, timestep, norm_gain, time_weight, conv_weight, attend_weight, output_weight):
    features = sinusoid(timestep).astype(jnp.bfloat16)
    time_bias = jnp.dot(features, time_weight, preferred_element_type=jnp.float32)

    def one_clip(packed):
        clip, bias_row = packed
        values = clip.astype(jnp.float32)
        grouped = values.reshape(FRAMES, PIX, GROUPS, C // GROUPS)
        center = lax.optimization_barrier(jnp.mean(grouped, axis=(0, 1, 3)))
        spread = lax.optimization_barrier(jnp.mean((grouped - center[None, None, :, None]) ** 2, axis=(0, 1, 3)))
        normed_group = (grouped - center[None, None, :, None]) / jnp.sqrt(spread[None, None, :, None] + 1e-05)
        scaled = normed_group.reshape(FRAMES, PIX, C) * norm_gain
        hidden = jax.nn.silu(scaled).astype(jnp.bfloat16)
        padded = jnp.pad(hidden, ((1, 1), (0, 0), (0, 0)))
        conv = jnp.zeros((FRAMES * PIX, C), jnp.float32)
        for offset in range(3):
            window = padded[offset:offset + FRAMES].reshape(FRAMES * PIX, C)
            conv = conv + jnp.dot(window, conv_weight[offset], preferred_element_type=jnp.float32)
        conv = conv + bias_row[None, :]
        residual = (values.reshape(FRAMES * PIX, C) + conv).astype(jnp.bfloat16)
        rows = residual.astype(jnp.float32)
        row_mean = lax.optimization_barrier(jnp.mean(rows, axis=-1, keepdims=True))
        row_var = lax.optimization_barrier(jnp.mean((rows - row_mean) ** 2, axis=-1, keepdims=True))
        normed = ((rows - row_mean) / jnp.sqrt(row_var + 1e-05)).astype(jnp.bfloat16)
        triple = jnp.dot(normed, attend_weight, preferred_element_type=jnp.float32).astype(jnp.bfloat16)
        triple = triple.astype(jnp.float32).reshape(FRAMES, PIX, 3, HEADS, HD)
        queries = triple[:, :, 0]
        key_part = triple[:, :, 1]
        value_part = triple[:, :, 2]
        scores = jnp.einsum('fphd,gphd->phfg', queries, key_part) / math.sqrt(HD)
        peak = lax.optimization_barrier(jnp.max(scores, axis=-1, keepdims=True))
        expo = jnp.exp(scores - peak)
        probs = (expo / lax.optimization_barrier(jnp.sum(expo, axis=-1, keepdims=True))).astype(jnp.bfloat16)
        attended = jnp.einsum('phfg,gphd->fphd', probs.astype(jnp.float32), value_part)
        attended = attended.astype(jnp.bfloat16).reshape(FRAMES * PIX, C)
        mixed = rows + jnp.dot(attended, output_weight, preferred_element_type=jnp.float32)
        return mixed.astype(jnp.bfloat16).reshape(FRAMES, PIX, C)
    return lax.map(one_clip, (latents, time_bias))
```

```python
import functools
import math

import jax
import jax.numpy as jnp
import numpy as np
from jax import lax
from jax.experimental import pallas as pl
from jax.experimental.pallas import tpu as pltpu
from jax.sharding import PartitionSpec as P

HEADS = 20
HD = 64
GROUPS = 32
TEMB = 320


def with_halo(array, sides, width):
    for axis, dim in sides:
        count, length = (lax.axis_size(axis), array.shape[dim])
        up = [(i, (i + 1) % count) for i in range(count - 1)]
        down = [(j, i) for i, j in up]
        last = lax.slice_in_dim(array, length - width, length, axis=dim)
        initial = lax.slice_in_dim(array, 0, width, axis=dim)
        before = lax.ppermute(last, axis, up)
        after = lax.ppermute(initial, axis, down)
        array = jnp.concatenate([before, array, after], axis=dim)
    return array


def sinusoid(timestep):
    half_dim = TEMB // 2
    ladder = jnp.arange(half_dim, dtype=jnp.float32)
    freqs = jnp.exp(-math.log(10000.0) * ladder / half_dim)
    angles = timestep.astype(jnp.float32)[:, None] * freqs[None, :]
    return jnp.concatenate([jnp.cos(angles), jnp.sin(angles)], axis=-1)


def attend_pixels(triple):
    count_items, frames_all, pixels_here, width_three = triple.shape
    channels = width_three // 3
    parts = triple.reshape(count_items, frames_all, pixels_here, 3, HEADS, HD)
    queries = parts[:, :, :, 0]
    key_part = parts[:, :, :, 1]
    value_part = parts[:, :, :, 2]
    scores = jnp.einsum(
        "nfphd,ngphd->nphfg", queries, key_part, preferred_element_type=jnp.float32
    ) / math.sqrt(HD)
    peak = jnp.max(scores, axis=-1, keepdims=True)
    expo = jnp.exp(scores - peak)
    probs = (expo / jnp.sum(expo, axis=-1, keepdims=True)).astype(jnp.bfloat16)
    attended = jnp.einsum(
        "nphfg,ngphd->nfphd", probs, value_part, preferred_element_type=jnp.float32
    )
    attended = attended.astype(jnp.bfloat16).reshape(count_items, frames_all, pixels_here, channels)
    return lax.all_to_all(attended, "frame", split_axis=1, concat_axis=2, tiled=True)


def shards(latents, timestep, norm_gain, time_weight, conv_weight, attend_weight, output_weight):
    count_clips, frames_dev, pixels, channels = latents.shape
    group_width = channels // GROUPS
    time_full = lax.all_gather(time_weight, "dp", axis=0, tiled=True)
    features = sinusoid(timestep).astype(jnp.bfloat16)
    time_bias = jnp.dot(features, time_full, preferred_element_type=jnp.float32)
    conv_full, attend_full, output_full = (
        lax.all_gather(conv_weight, ("dp", "frame"), axis=1, tiled=True),
        lax.all_gather(attend_weight, ("dp", "frame"), axis=0, tiled=True),
        lax.all_gather(output_weight, ("dp", "frame"), axis=0, tiled=True),
    )
    values = latents.astype(jnp.float32)
    grouped = values.reshape(count_clips, frames_dev, pixels, GROUPS, group_width)
    members = frames_dev * lax.axis_size("frame") * pixels * group_width
    center = lax.psum(jnp.sum(grouped, axis=(1, 2, 4)), "frame") / members
    deviate = grouped - center[:, None, None, :, None]
    spread = lax.psum(jnp.sum(deviate * deviate, axis=(1, 2, 4)), "frame") / members
    normed_group = deviate / jnp.sqrt(spread[:, None, None, :, None] + 1e-05)
    scaled = normed_group.reshape(count_clips, frames_dev, pixels, channels) * norm_gain
    hidden = jax.nn.silu(scaled).astype(jnp.bfloat16)
    padded = with_halo(hidden, (("frame", 1),), 1)
    windows = [padded[:, offset : offset + frames_dev].reshape(-1, channels) for offset in range(3)]
    conv_init = jnp.zeros((count_clips * frames_dev * pixels, channels), jnp.float32)
    conv = conv_init
    for offset in range(3):
        conv = conv + jnp.dot(
            windows[offset], conv_full[offset], preferred_element_type=jnp.float32
        )
    conv = conv.reshape(count_clips, frames_dev, pixels, channels) + time_bias[:, None, None, :]
    residual = (values + conv).astype(jnp.bfloat16)
    rows = residual.astype(jnp.float32)
    row_mean = jnp.mean(rows, axis=-1, keepdims=True)
    row_var = jnp.mean((rows - row_mean) ** 2, axis=-1, keepdims=True)
    normed = ((rows - row_mean) / jnp.sqrt(row_var + 1e-05)).astype(jnp.bfloat16)
    product = jnp.dot(normed.reshape(-1, channels), attend_full, preferred_element_type=jnp.float32)
    triple = product.astype(jnp.bfloat16).reshape(count_clips, frames_dev, pixels, 3 * channels)
    attended = attend_pixels(
        lax.all_to_all(triple, "frame", split_axis=2, concat_axis=1, tiled=True)
    )
    flat_attended = attended.reshape(-1, channels)
    projected = jnp.dot(flat_attended, output_full, preferred_element_type=jnp.float32)
    mixed = rows + projected.reshape(count_clips, frames_dev, pixels, channels)
    return mixed.astype(jnp.bfloat16)


F32 = jnp.float32
BF16 = jnp.bfloat16
HPAD = 384


def split_rows(row):
    hi = row.astype(BF16).astype(F32)
    mid = (row - hi).astype(BF16).astype(F32)
    low = row - hi - mid
    place = lax.broadcasted_iota(jnp.int32, (16, row.shape[1]), 0)
    both = jnp.where(place == 0, hi, jnp.where(place == 1, mid, jnp.where(place == 2, low, 0.0)))
    return both.astype(BF16)


def group_mean(row, ind, ind_back, count):
    sums = jnp.dot(split_rows(row), ind, preferred_element_type=F32)
    sums = jnp.sum(sums, axis=0, keepdims=True) / count
    wide = jnp.dot(split_rows(sums), ind_back, preferred_element_type=F32)
    return jnp.sum(wide, axis=0, keepdims=True)


def kernel(
    planes, dps, lat_ref, feat_ref, gain_ref, time_ref, conv_ref, att_ref, outw_ref,
    ind_ref, indb_ref, e_ref, et_ref, out_ref,
    L, H, S1, S2, A1, A2, GC, GA, Y, RS, Q, K, V, ATS, AT, WO,
    lat_s, lat_r, a_s, a_r, g_s, g_r, rs_s, rs_r, at_s, at_r, wo_s, wo_r, wf_s,
):
    d = lax.axis_index("dp")
    f = lax.axis_index("frame")
    z = d // 2
    c = d % 2
    sib = d + 1 - 2 * c
    levels = dps // 2
    frames, pixels, channels = L.shape
    mine = frames // planes
    cols = channels // planes
    depth = conv_ref.shape[1]
    block = planes * depth

    barrier = pltpu.get_barrier_semaphore()
    for j in range(1, planes):
        pl.semaphore_signal(barrier, inc=1, device_id={"frame": lax.rem(f + j, planes)}, device_id_type=pl.DeviceIdType.MESH)
    for j in range(1, dps):
        pl.semaphore_signal(barrier, inc=1, device_id={"dp": lax.rem(d + j, dps)}, device_id_type=pl.DeviceIdType.MESH)

    zeros8 = jnp.zeros((8, 3 * cols), F32)
    zeros8b = jnp.zeros((8, 4 * cols), F32)
    for j in range(planes):
        part = slice(j * cols, (j + 1) * cols)
        taps = [conv_ref[t].astype(F32)[:, part] for t in range(3)]
        S1[j] = jnp.concatenate([jnp.concatenate(taps, axis=1), zeros8], axis=0).astype(BF16)
        att = att_ref[...].astype(F32)
        quads = [att[:, t * channels + j * cols : t * channels + (j + 1) * cols] for t in range(3)]
        quads.append(outw_ref[...].astype(F32)[:, part])
        S2[j] = jnp.concatenate([jnp.concatenate(quads, axis=1), zeros8b], axis=0).astype(BF16)
    pl.semaphore_wait(barrier, planes - 1 + dps - 1)

    def remote(src, dst, ss, rs, where):
        return pltpu.make_async_remote_copy(
            src_ref=src, dst_ref=dst, send_sem=ss, recv_sem=rs, device_id=where,
            device_id_type=pl.DeviceIdType.MESH,
        )

    def peer(j):
        return lax.rem(f + j, planes)

    def source(j):
        return lax.rem(f + planes - j, planes)

    my_frames = pl.ds(f * mine, mine)

    def a_copy(k, j):
        src, dst = ((S1, A1), (S2, A2))[k]
        p = peer(j)
        return remote(src.at[p], dst.at[f], a_s.at[k, j], a_r.at[k, j], {"frame": p})

    def lat_copy(j):
        return remote(lat_ref, L.at[my_frames], lat_s.at[j], lat_r.at[j], {"frame": peer(j)})

    for j in range(1, planes):
        a_copy(0, j).start()
    for j in range(1, planes):
        lat_copy(j).start()
    for j in range(1, planes):
        a_copy(1, j).start()
    L[my_frames] = lat_ref[...]
    A1[f] = S1[f]
    A2[f] = S2[f]

    def stack(buf):
        return jnp.concatenate([buf[j].astype(F32)[:depth] for j in range(planes)], axis=0)

    G = (GC, GA)

    def g_copy(k, owner, slot, target):
        return remote(G[k].at[owner], G[k].at[owner], g_s.at[k, slot], g_r.at[k, owner], {"dp": target})

    def guarded(cond, fn):
        pl.when(cond)(fn)

    def push(k, owner, step, right, left, act):
        if right is not None:
            guarded(right, lambda: act(g_copy(k, owner, 3 * step, d + 2)))
        if left is not None:
            guarded(left, lambda: act(g_copy(k, owner, 3 * step + 1, d - 2)))
        return None

    def steps_of(k, step, act):
        if step == 0:
            guarded(z < levels - 1, lambda: act(0, d, 0, d + 2))
            guarded(z > 0, lambda: act(0, d, 1, d - 2))
            act(0, d, 2, sib)
            return
        below = d - 2 * step
        above = d + 2 * step
        base = 4 * step - 1

        @pl.when(z >= step)
        def _():
            act(1, below, 0, sib)
            guarded(z < levels - 1, lambda: act(0, below, base, d + 2))
            act(0, below, base + 1, sib)

        @pl.when(z + step < levels)
        def _():
            act(1, above, 0, sib)
            guarded(z > 0, lambda: act(0, above, base + 2, d - 2))
            act(0, above, base + 3, sib)

    def relay(k, step):
        def act(kind, owner, slot, target):
            copy = g_copy(k, owner, slot, target)
            if kind == 1:
                copy.wait_recv()
            else:
                copy.start()

        steps_of(k, step, act)

    def drain(k):
        def act(kind, owner, slot, target):
            if kind == 0:
                g_copy(k, owner, slot, target).wait_send()

        for step in range(levels):
            steps_of(k, step, act)

    def from_sibling(k):
        for zz in range(levels):
            g_copy(k, 2 * zz + 1 - c, 0, sib).wait_recv()

    for j in range(1, planes):
        a_copy(0, j).wait_recv()
    GC[d, 0:block] = stack(A1).astype(BF16)
    GC[d, block : block + 16] = time_ref[...]
    relay(0, 0)
    for j in range(1, planes):
        a_copy(1, j).wait_recv()
    GA[d] = stack(A2).astype(BF16)
    for step in range(1, levels):
        relay(0, step)
    relay(1, 0)

    for j in range(1, planes):
        lat_copy(j).wait_recv()

    def fold(rows):
        return jnp.sum(rows.reshape(pixels // 8, 8, channels), axis=0)

    def sum_frame(i, acc):
        return acc + fold(L[i].astype(F32))

    start = jnp.zeros((8, channels), F32)
    total = lax.fori_loop(0, frames, sum_frame, start)
    count = float(frames * pixels * (channels // GROUPS))
    ind, indb = ind_ref[...], indb_ref[...]
    center = group_mean(jnp.sum(total, axis=0, keepdims=True), ind, indb, count)

    def dev_frame(i, acc):
        dev = L[i].astype(F32) - center
        return acc + fold(dev * dev)

    total2 = lax.fori_loop(0, frames, dev_frame, start)
    spread = group_mean(jnp.sum(total2, axis=0, keepdims=True), ind, indb, count)
    scale = gain_ref[...] / jnp.sqrt(spread + 1e-05)

    def hide_frame(i, carry):
        scaled = (L[i].astype(F32) - center) * scale
        H[i] = (scaled / (1.0 + jnp.exp(-scaled))).astype(BF16)
        return carry

    lax.fori_loop(0, frames, hide_frame, 0)
    relay(1, 1)

    from_sibling(0)
    Y[0] = jnp.zeros(Y.shape[1:], F32)
    Y[frames + 1] = jnp.zeros(Y.shape[1:], F32)

    def conv_pair(i, carry):
        rows = H[pl.ds(2 * i, 2)].reshape(2 * pixels, channels)
        weight = GC[:, 0:block, :].reshape(dps * block, 3 * cols)
        y = jnp.dot(rows, weight, preferred_element_type=F32)
        Y[pl.ds(2 * i + 1, 2)] = y.reshape(2, pixels, 3 * cols)
        return carry

    lax.fori_loop(0, frames // 2, conv_pair, 0)
    times = GC[:, block : block + 16, :].reshape(dps * 16, 3 * cols)
    tb = jnp.dot(feat_ref[...], times, preferred_element_type=F32)
    bias = tb[0:1, 0:cols] + tb[1:2, cols : 2 * cols] + tb[2:3, 2 * cols : 3 * cols]

    def res_frame(i, carry):
        conv = Y[i][:, 0:cols] + Y[i + 1][:, cols : 2 * cols] + Y[i + 2][:, 2 * cols : 3 * cols]
        x = L[i].astype(F32)
        own = x[:, 0:cols]
        for j in range(1, planes):
            own = jnp.where(f == j, x[:, j * cols : (j + 1) * cols], own)
        RS[f, i] = (own + (conv + bias)).astype(BF16)
        return carry

    lax.fori_loop(0, frames, res_frame, 0)

    def rs_copy(j):
        return remote(RS.at[f], RS.at[f], rs_s.at[j], rs_r.at[j], {"frame": peer(j)})

    for j in range(1, planes):
        rs_copy(j).start()
    for step in range(2, levels):
        relay(1, step)
    from_sibling(1)

    half = dps * block // 2
    WO[f] = GA[:, :, 3 * cols : 4 * cols].reshape(dps * block, cols)

    def wo_copy(j):
        part = pl.ds(pl.multiple_of(c * half, 16), half)
        return remote(WO.at[f, part], WO.at[f, part], wo_s.at[j], wo_r.at[j, 0], {"frame": peer(j)})

    def wo_share(j):
        part = pl.ds(pl.multiple_of(c * half, 16), half)
        s = source(j)
        return remote(WO.at[s, part], WO.at[s, part], wf_s.at[j], wo_r.at[j, 1], {"dp": sib})

    for j in range(1, planes):
        rs_copy(j).wait_recv()
    for j in range(1, planes):
        wo_copy(j).start()

    def rows_of(i):
        return jnp.concatenate([RS[j, i].astype(F32) for j in range(planes)], axis=1)

    def norm_frame(i, carry):
        rows = rows_of(i)
        mean = jnp.mean(rows, axis=-1, keepdims=True)
        dev = rows - mean
        var = jnp.mean(dev * dev, axis=-1, keepdims=True)
        H[i] = (dev / jnp.sqrt(var + 1e-05)).astype(BF16)
        return carry

    lax.fori_loop(0, frames, norm_frame, 0)
    pad = jnp.zeros((pixels, HPAD - cols), F32)

    def triple_pair(i, carry):
        rows = H[pl.ds(2 * i, 2)].reshape(2 * pixels, channels)
        weight = GA[:, :, 0 : 3 * cols].reshape(dps * block, 3 * cols)
        y = jnp.dot(rows, weight, preferred_element_type=F32)
        for n in range(2):
            for t, buf in enumerate((Q, K, V)):
                piece = y[n * pixels : (n + 1) * pixels, t * cols : (t + 1) * cols]
                buf[2 * i + n] = jnp.concatenate([piece, pad], axis=1).astype(BF16)
        return carry

    lax.fori_loop(0, frames // 2, triple_pair, 0)

    def attend(i, carry):
        q = Q[i]
        prods = jnp.concatenate([q * K[g] for g in range(frames)], axis=1)
        scores = jnp.dot(prods, e_ref[...], preferred_element_type=F32) * (1.0 / math.sqrt(HD))
        peak = scores
        for shift in (8, 16, 32):
            peak = jnp.maximum(peak, pltpu.roll(peak, shift, 1))
        expo = jnp.exp(scores - peak)
        total = expo
        for shift in (8, 16, 32):
            total = total + pltpu.roll(total, shift, 1)
        probs = (expo / total).astype(BF16)
        spreads = jnp.dot(probs, et_ref[...], preferred_element_type=F32)
        acc = spreads[:, 0:HPAD] * V[0].astype(F32)
        for g in range(1, frames):
            acc = acc + spreads[:, g * HPAD : (g + 1) * HPAD] * V[g].astype(F32)
        ATS[i] = acc[:, 0:cols].astype(BF16)
        return carry

    lax.fori_loop(0, frames, attend, 0)

    def at_copy(j):
        p = peer(j)
        return remote(ATS.at[pl.ds(p * mine, mine)], AT.at[f], at_s.at[j], at_r.at[j], {"frame": p})

    for j in range(1, planes):
        at_copy(j).start()
    AT[f] = ATS[my_frames]
    for j in range(1, planes):
        wo_copy(j).wait_recv()
        wo_share(j).start()
    for j in range(1, planes):
        wo_share(j).wait_recv()
    for j in range(1, planes):
        at_copy(j).wait_recv()

    def out_frame(i, carry):
        a = jnp.concatenate([AT[j, i].astype(F32) for j in range(planes)], axis=1).astype(BF16)
        parts = [jnp.dot(a, WO[j], preferred_element_type=F32) for j in range(planes)]
        mixed = rows_of(f * mine + i) + jnp.concatenate(parts, axis=1)
        out_ref[i] = mixed.astype(BF16)
        return carry

    lax.fori_loop(0, mine, out_frame, 0)

    for j in range(1, planes):
        a_copy(0, j).wait_send()
        a_copy(1, j).wait_send()
        lat_copy(j).wait_send()
        rs_copy(j).wait_send()
        wo_copy(j).wait_send()
        wo_share(j).wait_send()
        at_copy(j).wait_send()
    drain(0)
    drain(1)


def indicators(frames, channels, cols):
    group = np.arange(channels) // (channels // GROUPS)
    ind = (group[:, None] == np.arange(128)[None, :]).astype(np.float32)
    row = np.arange(frames * HPAD)
    item, head = row // HPAD, (row % HPAD) // HD
    lane = np.arange(128)
    hit = (item[:, None] == (lane % 64)[None, :] // 8) & (head[:, None] == lane[None, :] % 8)
    hit = hit & (head < cols // HD)[:, None]
    back = (hit & (lane < 64)[None, :]).T
    return [jnp.asarray(m, BF16) for m in (ind, ind.T, hit.astype(np.float32), back.astype(np.float32))]


def fast_shards(latents, timestep, norm_gain, time_weight, conv_weight, attend_weight, output_weight):
    planes, dps = lax.axis_size("frame"), lax.axis_size("dp")
    _, mine, pixels, channels = latents.shape
    frames = mine * planes
    cols = channels // planes
    depth = conv_weight.shape[1]
    block = depth * planes
    f = lax.axis_index("frame")
    rows = time_weight.shape[0]
    features = sinusoid(timestep).astype(BF16).reshape(dps, rows)
    features = jnp.pad(features, ((0, 0), (0, 48 - rows))).reshape(dps, 3, 16)
    feats = jnp.pad(features.transpose(1, 0, 2).reshape(3, dps * 16), ((0, 13), (0, 0)))
    times = lax.dynamic_slice_in_dim(time_weight, f * cols, cols, axis=1)
    times = jnp.pad(times, ((0, 48 - rows), (0, 0))).reshape(3, 16, cols)
    times = times.transpose(1, 0, 2).reshape(16, 3 * cols)
    ind, indb, e, et = indicators(frames, channels, cols)
    vmem = pl.BlockSpec(memory_space=pltpu.VMEM)
    DMA = pltpu.SemaphoreType.DMA
    slots = 4 * (dps // 2)
    out = pl.pallas_call(
        functools.partial(kernel, planes, dps),
        out_shape=jax.ShapeDtypeStruct((mine, pixels, channels), BF16),
        in_specs=[vmem] * 11,
        out_specs=vmem,
        scratch_shapes=[
            pltpu.VMEM((frames, pixels, channels), BF16),
            pltpu.VMEM((frames, pixels, channels), BF16),
            pltpu.VMEM((planes, depth + 8, 3 * cols), BF16),
            pltpu.VMEM((planes, depth + 8, 4 * cols), BF16),
            pltpu.VMEM((planes, depth + 8, 3 * cols), BF16),
            pltpu.VMEM((planes, depth + 8, 4 * cols), BF16),
            pltpu.VMEM((dps, block + 16, 3 * cols), BF16),
            pltpu.VMEM((dps, block, 4 * cols), BF16),
            pltpu.VMEM((frames + 2, pixels, 3 * cols), F32),
            pltpu.VMEM((planes, frames, pixels, cols), BF16),
            pltpu.VMEM((frames, pixels, HPAD), BF16),
            pltpu.VMEM((frames, pixels, HPAD), BF16),
            pltpu.VMEM((frames, pixels, HPAD), BF16),
            pltpu.VMEM((frames, pixels, cols), BF16),
            pltpu.VMEM((planes, mine, pixels, cols), BF16),
            pltpu.VMEM((planes, dps * block, cols), BF16),
            DMA((planes,)), DMA((planes,)),
            DMA((2, planes)), DMA((2, planes)),
            DMA((2, slots)), DMA((2, dps)),
            DMA((planes,)), DMA((planes,)),
            DMA((planes,)), DMA((planes,)),
            DMA((planes,)), DMA((planes, 2)), DMA((planes,)),
        ],
        compiler_params=pltpu.CompilerParams(
            collective_id=0, has_side_effects=True, vmem_limit_bytes=56 * 1024 * 1024
        ),
        cost_estimate=pl.CostEstimate(flops=7_000_000_000, bytes_accessed=8_000_000, transcendentals=3_000_000),
    )(
        latents[0], feats, norm_gain[None, :], times, conv_weight, attend_weight, output_weight,
        ind, indb, e, et,
    )
    return out[None]


def fits(mesh):
    planes, dps = mesh.shape["frame"], mesh.shape["dp"]
    return planes == 4 and dps == 8


def solution(mesh):
    in_specs = (
        P("dp", "frame", None, None),
        P("dp"),
        P(),
        P("dp", None),
        P(None, ("dp", "frame"), None),
        P(("dp", "frame"), None),
        P(("dp", "frame"), None),
    )
    out_specs = P("dp", "frame", None, None)
    return jax.shard_map(fast_shards if fits(mesh) else shards, mesh=mesh, in_specs=in_specs, out_specs=out_specs, check_vma=False)
```

```python
import functools
import math

import jax
import jax.numpy as jnp
import numpy as np
from jax import lax
from jax.experimental import pallas as pl
from jax.experimental.pallas import tpu as pltpu
from jax.sharding import PartitionSpec as P

HEADS = 20
HD = 64
GROUPS = 32
TEMB = 320


def with_halo(array, sides, width):
    for axis, dim in sides:
        count, length = (lax.axis_size(axis), array.shape[dim])
        up = [(i, (i + 1) % count) for i in range(count - 1)]
        down = [(j, i) for i, j in up]
        last = lax.slice_in_dim(array, length - width, length, axis=dim)
        initial = lax.slice_in_dim(array, 0, width, axis=dim)
        before = lax.ppermute(last, axis, up)
        after = lax.ppermute(initial, axis, down)
        array = jnp.concatenate([before, array, after], axis=dim)
    return array


def sinusoid(timestep):
    half_dim = TEMB // 2
    ladder = jnp.arange(half_dim, dtype=jnp.float32)
    freqs = jnp.exp(-math.log(10000.0) * ladder / half_dim)
    angles = timestep.astype(jnp.float32)[:, None] * freqs[None, :]
    return jnp.concatenate([jnp.cos(angles), jnp.sin(angles)], axis=-1)


def attend_pixels(triple):
    count_items, frames_all, pixels_here, width_three = triple.shape
    channels = width_three // 3
    parts = triple.reshape(count_items, frames_all, pixels_here, 3, HEADS, HD)
    queries = parts[:, :, :, 0]
    key_part = parts[:, :, :, 1]
    value_part = parts[:, :, :, 2]
    scores = jnp.einsum(
        "nfphd,ngphd->nphfg", queries, key_part, preferred_element_type=jnp.float32
    ) / math.sqrt(HD)
    peak = jnp.max(scores, axis=-1, keepdims=True)
    expo = jnp.exp(scores - peak)
    probs = (expo / jnp.sum(expo, axis=-1, keepdims=True)).astype(jnp.bfloat16)
    attended = jnp.einsum(
        "nphfg,ngphd->nfphd", probs, value_part, preferred_element_type=jnp.float32
    )
    attended = attended.astype(jnp.bfloat16).reshape(count_items, frames_all, pixels_here, channels)
    return lax.all_to_all(attended, "frame", split_axis=1, concat_axis=2, tiled=True)


def shards(latents, timestep, norm_gain, time_weight, conv_weight, attend_weight, output_weight):
    count_clips, frames_dev, pixels, channels = latents.shape
    group_width = channels // GROUPS
    time_full = lax.all_gather(time_weight, "dp", axis=0, tiled=True)
    features = sinusoid(timestep).astype(jnp.bfloat16)
    time_bias = jnp.dot(features, time_full, preferred_element_type=jnp.float32)
    conv_full, attend_full, output_full = (
        lax.all_gather(conv_weight, ("dp", "frame"), axis=1, tiled=True),
        lax.all_gather(attend_weight, ("dp", "frame"), axis=0, tiled=True),
        lax.all_gather(output_weight, ("dp", "frame"), axis=0, tiled=True),
    )
    values = latents.astype(jnp.float32)
    grouped = values.reshape(count_clips, frames_dev, pixels, GROUPS, group_width)
    members = frames_dev * lax.axis_size("frame") * pixels * group_width
    center = lax.psum(jnp.sum(grouped, axis=(1, 2, 4)), "frame") / members
    deviate = grouped - center[:, None, None, :, None]
    spread = lax.psum(jnp.sum(deviate * deviate, axis=(1, 2, 4)), "frame") / members
    normed_group = deviate / jnp.sqrt(spread[:, None, None, :, None] + 1e-05)
    scaled = normed_group.reshape(count_clips, frames_dev, pixels, channels) * norm_gain
    hidden = jax.nn.silu(scaled).astype(jnp.bfloat16)
    padded = with_halo(hidden, (("frame", 1),), 1)
    windows = [padded[:, offset : offset + frames_dev].reshape(-1, channels) for offset in range(3)]
    conv_init = jnp.zeros((count_clips * frames_dev * pixels, channels), jnp.float32)
    conv = conv_init
    for offset in range(3):
        conv = conv + jnp.dot(
            windows[offset], conv_full[offset], preferred_element_type=jnp.float32
        )
    conv = conv.reshape(count_clips, frames_dev, pixels, channels) + time_bias[:, None, None, :]
    residual = (values + conv).astype(jnp.bfloat16)
    rows = residual.astype(jnp.float32)
    row_mean = jnp.mean(rows, axis=-1, keepdims=True)
    row_var = jnp.mean((rows - row_mean) ** 2, axis=-1, keepdims=True)
    normed = ((rows - row_mean) / jnp.sqrt(row_var + 1e-05)).astype(jnp.bfloat16)
    product = jnp.dot(normed.reshape(-1, channels), attend_full, preferred_element_type=jnp.float32)
    triple = product.astype(jnp.bfloat16).reshape(count_clips, frames_dev, pixels, 3 * channels)
    attended = attend_pixels(
        lax.all_to_all(triple, "frame", split_axis=2, concat_axis=1, tiled=True)
    )
    flat_attended = attended.reshape(-1, channels)
    projected = jnp.dot(flat_attended, output_full, preferred_element_type=jnp.float32)
    mixed = rows + projected.reshape(count_clips, frames_dev, pixels, channels)
    return mixed.astype(jnp.bfloat16)


F32 = jnp.float32
BF16 = jnp.bfloat16
HPAD = 384


def split_rows(row):
    hi = row.astype(BF16).astype(F32)
    mid = (row - hi).astype(BF16).astype(F32)
    low = row - hi - mid
    place = lax.broadcasted_iota(jnp.int32, (16, row.shape[1]), 0)
    both = jnp.where(place == 0, hi, jnp.where(place == 1, mid, jnp.where(place == 2, low, 0.0)))
    return both.astype(BF16)


def group_mean(row, ind, ind_back, count):
    sums = jnp.dot(split_rows(row), ind, preferred_element_type=F32)
    sums = jnp.sum(sums, axis=0, keepdims=True) / count
    wide = jnp.dot(split_rows(sums), ind_back, preferred_element_type=F32)
    return jnp.sum(wide, axis=0, keepdims=True)


def kernel(
    planes, dps, lat_ref, feat_ref, gain_ref, time_ref, conv_ref, att_ref, outw_ref,
    ind_ref, indb_ref, e_ref, et_ref, out_ref,
    L, H, S1, S2, A1, A2, GC, GA, Y, RS, Q, K, V, ATS, AT, WO,
    lat_s, lat_r, a_s, a_r, g_s, g_r, rs_s, rs_r, at_s, at_r, wo_s, wo_r, wf_s,
):
    d = lax.axis_index("dp")
    f = lax.axis_index("frame")
    z = d // 2
    c = d % 2
    sib = d + 1 - 2 * c
    levels = dps // 2
    frames, pixels, channels = L.shape
    mine = frames // planes
    cols = channels // planes
    depth = conv_ref.shape[1]
    block = planes * depth

    barrier = pltpu.get_barrier_semaphore()
    for j in range(1, planes):
        pl.semaphore_signal(barrier, inc=1, device_id={"frame": lax.rem(f + j, planes)}, device_id_type=pl.DeviceIdType.MESH)
    for j in range(1, dps):
        pl.semaphore_signal(barrier, inc=1, device_id={"dp": lax.rem(d + j, dps)}, device_id_type=pl.DeviceIdType.MESH)

    zeros3 = jnp.zeros((8, 3 * cols), F32)
    zeros4 = jnp.zeros((8, 4 * cols), F32)
    att = att_ref[...].astype(F32)
    outw = outw_ref[...].astype(F32)
    for j in range(planes):
        part = slice(j * cols, (j + 1) * cols)
        quads = [conv_ref[t].astype(F32)[:, part] for t in range(3)] + [outw[:, part]]
        S1[j] = jnp.concatenate([jnp.concatenate(quads, axis=1), zeros4], axis=0).astype(BF16)
        trio = [att[:, t * channels + j * cols : t * channels + (j + 1) * cols] for t in range(3)]
        S2[j] = jnp.concatenate([jnp.concatenate(trio, axis=1), zeros3], axis=0).astype(BF16)
    pl.semaphore_wait(barrier, planes - 1 + dps - 1)

    def remote(src, dst, ss, rs, where):
        return pltpu.make_async_remote_copy(
            src_ref=src, dst_ref=dst, send_sem=ss, recv_sem=rs, device_id=where,
            device_id_type=pl.DeviceIdType.MESH,
        )

    def peer(j):
        return lax.rem(f + j, planes)

    def source(j):
        return lax.rem(f + planes - j, planes)

    my_frames = pl.ds(f * mine, mine)

    def a_copy(k, j):
        src, dst = ((S1, A1), (S2, A2))[k]
        p = peer(j)
        return remote(src.at[p], dst.at[f], a_s.at[k, j], a_r.at[k, j], {"frame": p})

    side = [f + 1 - 2 * (f % 2), f + 2 - 4 * (f // 2)]
    diag = planes - 1 - f

    def lat_copy(n):
        return remote(lat_ref, L.at[my_frames], lat_s.at[n], lat_r.at[n], {"frame": side[n]})

    def lat_pass(n):
        part = pl.ds(side[n] * mine + n * (mine // 2), mine // 2)
        return remote(L.at[part], L.at[part], lat_s.at[2 + n], lat_r.at[2 + n], {"frame": side[1 - n]})

    for j in range(1, planes):
        a_copy(0, j).start()
    for n in range(2):
        lat_copy(n).start()
    for j in range(1, planes):
        a_copy(1, j).start()
    L[my_frames] = lat_ref[...]
    A1[f] = S1[f]
    A2[f] = S2[f]

    def stack(buf):
        return jnp.concatenate([buf[j].astype(F32)[:depth] for j in range(planes)], axis=0)

    G = (GC, GA)

    def g_copy(k, owner, slot, target):
        return remote(G[k].at[owner], G[k].at[owner], g_s.at[k, slot], g_r.at[k, owner], {"dp": target})

    def guarded(cond, fn):
        pl.when(cond)(fn)

    def steps_of(k, step, act):
        if step == 0:
            guarded(z < levels - 1, lambda: act(0, d, 0, d + 2))
            guarded(z > 0, lambda: act(0, d, 1, d - 2))
            act(0, d, 2, sib)
            return
        below = d - 2 * step
        above = d + 2 * step
        base = 4 * step - 1

        @pl.when(z >= step)
        def _():
            act(1, below, 0, sib)
            guarded(z < levels - 1, lambda: act(0, below, base, d + 2))
            act(0, below, base + 1, sib)

        @pl.when(z + step < levels)
        def _():
            act(1, above, 0, sib)
            guarded(z > 0, lambda: act(0, above, base + 2, d - 2))
            act(0, above, base + 3, sib)

    def relay(k, step):
        def act(kind, owner, slot, target):
            copy = g_copy(k, owner, slot, target)
            if kind == 1:
                copy.wait_recv()
            else:
                copy.start()

        steps_of(k, step, act)

    def drain(k):
        def act(kind, owner, slot, target):
            if kind == 0:
                g_copy(k, owner, slot, target).wait_send()

        for step in range(levels):
            steps_of(k, step, act)

    def from_sibling(k):
        for zz in range(levels):
            g_copy(k, 2 * zz + 1 - c, 0, sib).wait_recv()

    for j in range(1, planes):
        a_copy(0, j).wait_recv()
    GC[d, 0:block] = stack(A1).astype(BF16)
    GC[d, block : block + 16] = time_ref[...]
    relay(0, 0)
    for j in range(1, planes):
        a_copy(1, j).wait_recv()
    GA[d] = stack(A2).astype(BF16)
    relay(0, 1)
    for n in range(2):
        lat_copy(n).wait_recv()
        lat_pass(n).start()
    for step in range(2, levels - 1):
        relay(0, step)
    relay(1, 0)

    for n in range(2):
        lat_pass(n).wait_recv()

    def fold(rows):
        return jnp.sum(rows.reshape(pixels // 8, 8, channels), axis=0)

    def sum_frame(i, acc):
        return acc + fold(L[i].astype(F32))

    start = jnp.zeros((8, channels), F32)
    total = lax.fori_loop(0, frames, sum_frame, start)
    count = float(frames * pixels * (channels // GROUPS))
    ind, indb = ind_ref[...], indb_ref[...]
    center = group_mean(jnp.sum(total, axis=0, keepdims=True), ind, indb, count)

    def dev_frame(i, acc):
        dev = L[i].astype(F32) - center
        return acc + fold(dev * dev)

    total2 = lax.fori_loop(0, frames, dev_frame, start)
    spread = group_mean(jnp.sum(total2, axis=0, keepdims=True), ind, indb, count)
    scale = gain_ref[...] / jnp.sqrt(spread + 1e-05)

    def hide_frame(i, carry):
        scaled = (L[i].astype(F32) - center) * scale
        H[i] = (scaled / (1.0 + jnp.exp(-scaled))).astype(BF16)
        return carry

    relay(0, levels - 1)
    relay(1, 1)
    lax.fori_loop(0, frames, hide_frame, 0)

    from_sibling(0)
    Y[0] = jnp.zeros(Y.shape[1:], F32)
    Y[frames + 1] = jnp.zeros(Y.shape[1:], F32)

    half = dps * block // 2
    WO[f] = GC[:, 0:block, 3 * cols : 4 * cols].reshape(dps * block, cols)

    def wo_copy(j):
        part = pl.ds(pl.multiple_of(c * half, 16), half)
        return remote(WO.at[f, part], WO.at[f, part], wo_s.at[j], wo_r.at[j, 0], {"frame": peer(j)})

    def wo_share(j):
        part = pl.ds(pl.multiple_of(c * half, 16), half)
        t = source(j)
        return remote(WO.at[t, part], WO.at[t, part], wf_s.at[j], wo_r.at[j, 1], {"dp": sib})

    for j in range(1, planes):
        wo_copy(j).start()

    pairs = frames // 2

    def conv_pair(i):
        rows = H[2 * i : 2 * i + 2].reshape(2 * pixels, channels)
        weight = GC[:, 0:block, 0 : 3 * cols].reshape(dps * block, 3 * cols)
        y = jnp.dot(rows, weight, preferred_element_type=F32)
        Y[2 * i + 1 : 2 * i + 3] = y.reshape(2, pixels, 3 * cols)

    times = GC[:, block : block + 16, 0 : 3 * cols].reshape(dps * 16, 3 * cols)
    tb = jnp.dot(feat_ref[...], times, preferred_element_type=F32)
    bias = tb[0:1, 0:cols] + tb[1:2, cols : 2 * cols] + tb[2:3, 2 * cols : 3 * cols]

    def res_pair(p):
        both = []
        for i in (2 * p, 2 * p + 1):
            conv = Y[i][:, 0:cols] + Y[i + 1][:, cols : 2 * cols] + Y[i + 2][:, 2 * cols : 3 * cols]
            x = L[i].astype(F32)
            own = x[:, 0:cols]
            for j in range(1, planes):
                own = jnp.where(f == j, x[:, j * cols : (j + 1) * cols], own)
            both.append(own + (conv + bias))
        RS[f, p] = jnp.concatenate(both, axis=1).astype(BF16)

    def rs_copy(p, n):
        return remote(RS.at[f, p], RS.at[f, p], rs_s.at[p, n], rs_r.at[p, n], {"frame": side[n]})

    def rs_pass(p, n):
        part = pl.ds(n * (pixels // 2), pixels // 2)
        piece = RS.at[side[n], p, part]
        return remote(piece, piece, rs_s.at[p, 2 + n], rs_r.at[p, 2 + n], {"frame": side[1 - n]})

    def send_pair(p):
        res_pair(p)
        for n in range(2):
            rs_copy(p, n).start()

    def pass_pair(p):
        for n in range(2):
            rs_copy(p, n).wait_recv()
            rs_pass(p, n).start()

    conv_pair(0)
    for p in range(pairs):
        if p + 1 < pairs:
            conv_pair(p + 1)
        send_pair(p)
        if p == 0:
            for step in range(2, levels):
                relay(1, step)
        else:
            pass_pair(p - 1)
    from_sibling(1)

    def rows_of(p, n):
        return jnp.concatenate(
            [RS[j, p].astype(F32)[:, n * cols : (n + 1) * cols] for j in range(planes)], axis=1
        )

    def norm_pair(p):
        for n in range(2):
            rows = rows_of(p, n)
            mean = jnp.mean(rows, axis=-1, keepdims=True)
            dev = rows - mean
            var = jnp.mean(dev * dev, axis=-1, keepdims=True)
            H[2 * p + n] = (dev / jnp.sqrt(var + 1e-05)).astype(BF16)

    pad = jnp.zeros((pixels, HPAD - cols), F32)

    def triple_pair(i):
        rows = H[2 * i : 2 * i + 2].reshape(2 * pixels, channels)
        weight = GA[:, :, 0 : 3 * cols].reshape(dps * block, 3 * cols)
        y = jnp.dot(rows, weight, preferred_element_type=F32)
        for n in range(2):
            for t, buf in enumerate((Q, K, V)):
                piece = y[n * pixels : (n + 1) * pixels, t * cols : (t + 1) * cols]
                buf[2 * i + n] = jnp.concatenate([piece, pad], axis=1).astype(BF16)

    for p in range(pairs):
        if p == 0:
            pass_pair(pairs - 1)
        for n in range(2):
            rs_pass(p, n).wait_recv()
        norm_pair(p)
        triple_pair(p)
    for j in range(1, planes):
        wo_copy(j).wait_recv()
        wo_share(j).start()

    def attend(i):
        q = Q[i]
        prods = jnp.concatenate([q * K[g] for g in range(frames)], axis=1)
        scores = jnp.dot(prods, e_ref[...], preferred_element_type=F32) * (1.0 / math.sqrt(HD))
        peak = scores
        for shift in (8, 16, 32):
            peak = jnp.maximum(peak, pltpu.roll(peak, shift, 1))
        expo = jnp.exp(scores - peak)
        total = expo
        for shift in (8, 16, 32):
            total = total + pltpu.roll(total, shift, 1)
        probs = (expo / total).astype(BF16)
        spreads = jnp.dot(probs, et_ref[...], preferred_element_type=F32)
        acc = spreads[:, 0:HPAD] * V[0].astype(F32)
        for g in range(1, frames):
            acc = acc + spreads[:, g * HPAD : (g + 1) * HPAD] * V[g].astype(F32)
        return acc[:, 0:cols]

    def attend_pair(j, carry):
        p = peer(j)
        both = [attend(p * mine + n) for n in range(mine)]
        ATS[p] = jnp.concatenate(both, axis=1).astype(BF16)
        pl.when(j < planes)(lambda: at_copy(j).start())
        return carry

    def at_copy(j):
        p = peer(j)
        return remote(ATS.at[p], AT.at[f], at_s.at[j], at_r.at[j], {"frame": p})

    lax.fori_loop(1, planes + 1, attend_pair, 0)
    AT[f] = ATS[f]
    for j in range(1, planes):
        wo_share(j).wait_recv()
    for j in range(1, planes):
        at_copy(j).wait_recv()

    wide = []
    for n in range(mine):
        heads = [AT[j].astype(F32)[:, n * cols : (n + 1) * cols] for j in range(planes)]
        wide.append(jnp.concatenate(heads, axis=1).astype(BF16))
    a = jnp.concatenate(wide, axis=0)
    parts = [jnp.dot(a, WO[j], preferred_element_type=F32) for j in range(planes)]
    mixed = jnp.concatenate(parts, axis=1)
    for n in range(mine):
        out_ref[n] = (rows_of(f, n) + mixed[n * pixels : (n + 1) * pixels]).astype(BF16)

    for j in range(1, planes):
        a_copy(0, j).wait_send()
        a_copy(1, j).wait_send()
        wo_copy(j).wait_send()
        wo_share(j).wait_send()
        at_copy(j).wait_send()
    for n in range(2):
        lat_copy(n).wait_send()
        lat_pass(n).wait_send()
        for p in range(pairs):
            rs_copy(p, n).wait_send()
            rs_pass(p, n).wait_send()
    drain(0)
    drain(1)


def indicators(frames, channels, cols):
    group = np.arange(channels) // (channels // GROUPS)
    ind = (group[:, None] == np.arange(128)[None, :]).astype(np.float32)
    row = np.arange(frames * HPAD)
    item, head = row // HPAD, (row % HPAD) // HD
    lane = np.arange(128)
    hit = (item[:, None] == (lane % 64)[None, :] // 8) & (head[:, None] == lane[None, :] % 8)
    hit = hit & (head < cols // HD)[:, None]
    back = (hit & (lane < 64)[None, :]).T
    return [jnp.asarray(m, BF16) for m in (ind, ind.T, hit.astype(np.float32), back.astype(np.float32))]


def fast_shards(latents, timestep, norm_gain, time_weight, conv_weight, attend_weight, output_weight):
    planes, dps = lax.axis_size("frame"), lax.axis_size("dp")
    _, mine, pixels, channels = latents.shape
    frames = mine * planes
    cols = channels // planes
    depth = conv_weight.shape[1]
    block = depth * planes
    f = lax.axis_index("frame")
    rows = time_weight.shape[0]
    features = sinusoid(timestep).astype(BF16).reshape(dps, rows)
    features = jnp.pad(features, ((0, 0), (0, 48 - rows))).reshape(dps, 3, 16)
    feats = jnp.pad(features.transpose(1, 0, 2).reshape(3, dps * 16), ((0, 13), (0, 0)))
    times = lax.dynamic_slice_in_dim(time_weight, f * cols, cols, axis=1)
    times = jnp.pad(times, ((0, 48 - rows), (0, 0))).reshape(3, 16, cols)
    times = jnp.pad(times.transpose(1, 0, 2).reshape(16, 3 * cols), ((0, 0), (0, cols)))
    ind, indb, e, et = indicators(frames, channels, cols)
    vmem = pl.BlockSpec(memory_space=pltpu.VMEM)
    DMA = pltpu.SemaphoreType.DMA
    slots = 4 * (dps // 2)
    out = pl.pallas_call(
        functools.partial(kernel, planes, dps),
        out_shape=jax.ShapeDtypeStruct((mine, pixels, channels), BF16),
        in_specs=[vmem] * 11,
        out_specs=vmem,
        scratch_shapes=[
            pltpu.VMEM((frames, pixels, channels), BF16),
            pltpu.VMEM((frames, pixels, channels), BF16),
            pltpu.VMEM((planes, depth + 8, 4 * cols), BF16),
            pltpu.VMEM((planes, depth + 8, 3 * cols), BF16),
            pltpu.VMEM((planes, depth + 8, 4 * cols), BF16),
            pltpu.VMEM((planes, depth + 8, 3 * cols), BF16),
            pltpu.VMEM((dps, block + 16, 4 * cols), BF16),
            pltpu.VMEM((dps, block, 3 * cols), BF16),
            pltpu.VMEM((frames + 2, pixels, 3 * cols), F32),
            pltpu.VMEM((planes, frames // 2, pixels, 2 * cols), BF16),
            pltpu.VMEM((frames, pixels, HPAD), BF16),
            pltpu.VMEM((frames, pixels, HPAD), BF16),
            pltpu.VMEM((frames, pixels, HPAD), BF16),
            pltpu.VMEM((planes, pixels, 2 * cols), BF16),
            pltpu.VMEM((planes, pixels, 2 * cols), BF16),
            pltpu.VMEM((planes, dps * block, cols), BF16),
            DMA((4,)), DMA((4,)),
            DMA((2, planes)), DMA((2, planes)),
            DMA((2, slots)), DMA((2, dps)),
            DMA((frames // 2, 4)), DMA((frames // 2, 4)),
            DMA((planes,)), DMA((planes,)),
            DMA((planes,)), DMA((planes, 2)), DMA((planes,)),
        ],
        compiler_params=pltpu.CompilerParams(
            collective_id=0, has_side_effects=True, vmem_limit_bytes=56 * 1024 * 1024
        ),
        cost_estimate=pl.CostEstimate(flops=7_000_000_000, bytes_accessed=8_000_000, transcendentals=3_000_000),
    )(
        latents[0], feats, norm_gain[None, :], times, conv_weight, attend_weight, output_weight,
        ind, indb, e, et,
    )
    return out[None]


def fits(mesh):
    planes, dps = mesh.shape["frame"], mesh.shape["dp"]
    return planes == 4 and dps == 8


def solution(mesh):
    in_specs = (
        P("dp", "frame", None, None),
        P("dp"),
        P(),
        P("dp", None),
        P(None, ("dp", "frame"), None),
        P(("dp", "frame"), None),
        P(("dp", "frame"), None),
    )
    out_specs = P("dp", "frame", None, None)
    return jax.shard_map(fast_shards if fits(mesh) else shards, mesh=mesh, in_specs=in_specs, out_specs=out_specs, check_vma=False)
```

```python
import functools
import math

import jax
import jax.numpy as jnp
import numpy as np
from jax import lax
from jax.experimental import pallas as pl
from jax.experimental.pallas import tpu as pltpu
from jax.sharding import PartitionSpec as P

HEADS = 20
HD = 64
GROUPS = 32
TEMB = 320


def with_halo(array, sides, width):
    for axis, dim in sides:
        count, length = (lax.axis_size(axis), array.shape[dim])
        up = [(i, (i + 1) % count) for i in range(count - 1)]
        down = [(j, i) for i, j in up]
        last = lax.slice_in_dim(array, length - width, length, axis=dim)
        initial = lax.slice_in_dim(array, 0, width, axis=dim)
        before = lax.ppermute(last, axis, up)
        after = lax.ppermute(initial, axis, down)
        array = jnp.concatenate([before, array, after], axis=dim)
    return array


def sinusoid(timestep):
    half_dim = TEMB // 2
    ladder = jnp.arange(half_dim, dtype=jnp.float32)
    freqs = jnp.exp(-math.log(10000.0) * ladder / half_dim)
    angles = timestep.astype(jnp.float32)[:, None] * freqs[None, :]
    return jnp.concatenate([jnp.cos(angles), jnp.sin(angles)], axis=-1)


def attend_pixels(triple):
    count_items, frames_all, pixels_here, width_three = triple.shape
    channels = width_three // 3
    parts = triple.reshape(count_items, frames_all, pixels_here, 3, HEADS, HD)
    queries = parts[:, :, :, 0]
    key_part = parts[:, :, :, 1]
    value_part = parts[:, :, :, 2]
    scores = jnp.einsum(
        "nfphd,ngphd->nphfg", queries, key_part, preferred_element_type=jnp.float32
    ) / math.sqrt(HD)
    peak = jnp.max(scores, axis=-1, keepdims=True)
    expo = jnp.exp(scores - peak)
    probs = (expo / jnp.sum(expo, axis=-1, keepdims=True)).astype(jnp.bfloat16)
    attended = jnp.einsum(
        "nphfg,ngphd->nfphd", probs, value_part, preferred_element_type=jnp.float32
    )
    attended = attended.astype(jnp.bfloat16).reshape(count_items, frames_all, pixels_here, channels)
    return lax.all_to_all(attended, "frame", split_axis=1, concat_axis=2, tiled=True)


def shards(latents, timestep, norm_gain, time_weight, conv_weight, attend_weight, output_weight):
    count_clips, frames_dev, pixels, channels = latents.shape
    group_width = channels // GROUPS
    time_full = lax.all_gather(time_weight, "dp", axis=0, tiled=True)
    features = sinusoid(timestep).astype(jnp.bfloat16)
    time_bias = jnp.dot(features, time_full, preferred_element_type=jnp.float32)
    conv_full, attend_full, output_full = (
        lax.all_gather(conv_weight, ("dp", "frame"), axis=1, tiled=True),
        lax.all_gather(attend_weight, ("dp", "frame"), axis=0, tiled=True),
        lax.all_gather(output_weight, ("dp", "frame"), axis=0, tiled=True),
    )
    values = latents.astype(jnp.float32)
    grouped = values.reshape(count_clips, frames_dev, pixels, GROUPS, group_width)
    members = frames_dev * lax.axis_size("frame") * pixels * group_width
    center = lax.psum(jnp.sum(grouped, axis=(1, 2, 4)), "frame") / members
    deviate = grouped - center[:, None, None, :, None]
    spread = lax.psum(jnp.sum(deviate * deviate, axis=(1, 2, 4)), "frame") / members
    normed_group = deviate / jnp.sqrt(spread[:, None, None, :, None] + 1e-05)
    scaled = normed_group.reshape(count_clips, frames_dev, pixels, channels) * norm_gain
    hidden = jax.nn.silu(scaled).astype(jnp.bfloat16)
    padded = with_halo(hidden, (("frame", 1),), 1)
    windows = [padded[:, offset : offset + frames_dev].reshape(-1, channels) for offset in range(3)]
    conv_init = jnp.zeros((count_clips * frames_dev * pixels, channels), jnp.float32)
    conv = conv_init
    for offset in range(3):
        conv = conv + jnp.dot(
            windows[offset], conv_full[offset], preferred_element_type=jnp.float32
        )
    conv = conv.reshape(count_clips, frames_dev, pixels, channels) + time_bias[:, None, None, :]
    residual = (values + conv).astype(jnp.bfloat16)
    rows = residual.astype(jnp.float32)
    row_mean = jnp.mean(rows, axis=-1, keepdims=True)
    row_var = jnp.mean((rows - row_mean) ** 2, axis=-1, keepdims=True)
    normed = ((rows - row_mean) / jnp.sqrt(row_var + 1e-05)).astype(jnp.bfloat16)
    product = jnp.dot(normed.reshape(-1, channels), attend_full, preferred_element_type=jnp.float32)
    triple = product.astype(jnp.bfloat16).reshape(count_clips, frames_dev, pixels, 3 * channels)
    attended = attend_pixels(
        lax.all_to_all(triple, "frame", split_axis=2, concat_axis=1, tiled=True)
    )
    flat_attended = attended.reshape(-1, channels)
    projected = jnp.dot(flat_attended, output_full, preferred_element_type=jnp.float32)
    mixed = rows + projected.reshape(count_clips, frames_dev, pixels, channels)
    return mixed.astype(jnp.bfloat16)


F32 = jnp.float32
BF16 = jnp.bfloat16
HPAD = 384


def split_rows(row):
    hi = row.astype(BF16).astype(F32)
    mid = (row - hi).astype(BF16).astype(F32)
    low = row - hi - mid
    place = lax.broadcasted_iota(jnp.int32, (16, row.shape[1]), 0)
    both = jnp.where(place == 0, hi, jnp.where(place == 1, mid, jnp.where(place == 2, low, 0.0)))
    return both.astype(BF16)


def group_mean(row, ind, ind_back, count):
    sums = jnp.dot(split_rows(row), ind, preferred_element_type=F32)
    sums = jnp.sum(sums, axis=0, keepdims=True) / count
    wide = jnp.dot(split_rows(sums), ind_back, preferred_element_type=F32)
    return jnp.sum(wide, axis=0, keepdims=True)


def kernel(
    planes, dps, lat_ref, feat_ref, gain_ref, time_ref, conv_ref, att_ref, outw_ref,
    ind_ref, indb_ref, e_ref, et_ref, out_ref,
    L, H, S1, S2, A1, A2, GC, GA, Y, RS, Q, K, V, ATS, AT, WO,
    lat_s, lat_r, a_s, a_r, g_s, g_r, rs_s, rs_r, at_s, at_r, wo_s, wo_r, wf_s,
):
    d = lax.axis_index("dp")
    f = lax.axis_index("frame")
    z = d // 2
    c = d % 2
    sib = d + 1 - 2 * c
    levels = dps // 2
    frames, pixels, channels = L.shape
    mine = frames // planes
    cols = channels // planes
    depth = conv_ref.shape[1]
    block = planes * depth

    barrier = pltpu.get_barrier_semaphore()
    for j in range(1, planes):
        pl.semaphore_signal(barrier, inc=1, device_id={"frame": lax.rem(f + j, planes)}, device_id_type=pl.DeviceIdType.MESH)
    for j in range(1, dps):
        pl.semaphore_signal(barrier, inc=1, device_id={"dp": lax.rem(d + j, dps)}, device_id_type=pl.DeviceIdType.MESH)

    zeros3 = jnp.zeros((8, 3 * cols), F32)
    zeros4 = jnp.zeros((8, 4 * cols), F32)
    att = att_ref[...].astype(F32)
    outw = outw_ref[...].astype(F32)
    for j in range(planes):
        part = slice(j * cols, (j + 1) * cols)
        taps = [conv_ref[t].astype(F32)[:, part] for t in range(3)]
        S1[j] = jnp.concatenate([jnp.concatenate(taps, axis=1), zeros3], axis=0).astype(BF16)
        quads = [att[:, t * channels + j * cols : t * channels + (j + 1) * cols] for t in range(3)]
        quads.append(outw[:, part])
        S2[j] = jnp.concatenate([jnp.concatenate(quads, axis=1), zeros4], axis=0).astype(BF16)
    pl.semaphore_wait(barrier, planes - 1 + dps - 1)

    def remote(src, dst, ss, rs, where):
        return pltpu.make_async_remote_copy(
            src_ref=src, dst_ref=dst, send_sem=ss, recv_sem=rs, device_id=where,
            device_id_type=pl.DeviceIdType.MESH,
        )

    def peer(j):
        return lax.rem(f + j, planes)

    def source(j):
        return lax.rem(f + planes - j, planes)

    my_frames = pl.ds(f * mine, mine)

    def a_copy(k, j):
        src, dst = ((S1, A1), (S2, A2))[k]
        p = peer(j)
        return remote(src.at[p], dst.at[f], a_s.at[k, j], a_r.at[k, j], {"frame": p})

    side = [f + 1 - 2 * (f % 2), f + 2 - 4 * (f // 2)]
    diag = planes - 1 - f

    def lat_copy(n):
        return remote(lat_ref, L.at[my_frames], lat_s.at[n], lat_r.at[n], {"frame": side[n]})

    def lat_pass(n):
        part = pl.ds(side[n] * mine + n * (mine // 2), mine // 2)
        return remote(L.at[part], L.at[part], lat_s.at[2 + n], lat_r.at[2 + n], {"frame": side[1 - n]})

    for j in range(1, planes):
        a_copy(0, j).start()
    for n in range(2):
        lat_copy(n).start()
    for j in range(1, planes):
        a_copy(1, j).start()
    L[my_frames] = lat_ref[...]
    A1[f] = S1[f]
    A2[f] = S2[f]

    def stack(buf):
        return jnp.concatenate([buf[j].astype(F32)[:depth] for j in range(planes)], axis=0)

    G = (GC, GA)

    def g_copy(k, owner, slot, target):
        return remote(G[k].at[owner], G[k].at[owner], g_s.at[k, slot], g_r.at[k, owner], {"dp": target})

    def guarded(cond, fn):
        pl.when(cond)(fn)

    def steps_of(k, step, act):
        if step == 0:
            guarded(z < levels - 1, lambda: act(0, d, 0, d + 2))
            guarded(z > 0, lambda: act(0, d, 1, d - 2))
            act(0, d, 2, sib)
            return
        below = d - 2 * step
        above = d + 2 * step
        base = 4 * step - 1

        @pl.when(z >= step)
        def _():
            act(1, below, 0, sib)
            guarded(z < levels - 1, lambda: act(0, below, base, d + 2))
            act(0, below, base + 1, sib)

        @pl.when(z + step < levels)
        def _():
            act(1, above, 0, sib)
            guarded(z > 0, lambda: act(0, above, base + 2, d - 2))
            act(0, above, base + 3, sib)

    def relay(k, step):
        def act(kind, owner, slot, target):
            copy = g_copy(k, owner, slot, target)
            if kind == 1:
                copy.wait_recv()
            else:
                copy.start()

        steps_of(k, step, act)

    def drain(k):
        def act(kind, owner, slot, target):
            if kind == 0:
                g_copy(k, owner, slot, target).wait_send()

        for step in range(levels):
            steps_of(k, step, act)

    def from_sibling(k):
        for zz in range(levels):
            g_copy(k, 2 * zz + 1 - c, 0, sib).wait_recv()

    for j in range(1, planes):
        a_copy(0, j).wait_recv()
    GC[d, 0:block] = stack(A1).astype(BF16)
    GC[d, block : block + 16] = time_ref[...]
    relay(0, 0)
    for j in range(1, planes):
        a_copy(1, j).wait_recv()
    GA[d] = stack(A2).astype(BF16)
    relay(0, 1)
    for n in range(2):
        lat_copy(n).wait_recv()
        lat_pass(n).start()
    for step in range(2, levels - 1):
        relay(0, step)
    relay(1, 0)

    for n in range(2):
        lat_pass(n).wait_recv()

    def fold(rows):
        return jnp.sum(rows.reshape(pixels // 8, 8, channels), axis=0)

    def sum_frame(i, acc):
        return acc + fold(L[i].astype(F32))

    start = jnp.zeros((8, channels), F32)
    total = lax.fori_loop(0, frames, sum_frame, start)
    count = float(frames * pixels * (channels // GROUPS))
    ind, indb = ind_ref[...], indb_ref[...]
    center = group_mean(jnp.sum(total, axis=0, keepdims=True), ind, indb, count)

    def dev_frame(i, acc):
        dev = L[i].astype(F32) - center
        return acc + fold(dev * dev)

    total2 = lax.fori_loop(0, frames, dev_frame, start)
    spread = group_mean(jnp.sum(total2, axis=0, keepdims=True), ind, indb, count)
    scale = gain_ref[...] / jnp.sqrt(spread + 1e-05)

    def hide_frame(i, carry):
        scaled = (L[i].astype(F32) - center) * scale
        H[i] = (scaled / (1.0 + jnp.exp(-scaled))).astype(BF16)
        return carry

    relay(0, levels - 1)
    relay(1, 1)
    lax.fori_loop(0, frames, hide_frame, 0)

    from_sibling(0)
    Y[0] = jnp.zeros(Y.shape[1:], F32)
    Y[frames + 1] = jnp.zeros(Y.shape[1:], F32)

    pairs = frames // 2

    def conv_pair(i):
        rows = H[2 * i : 2 * i + 2].reshape(2 * pixels, channels)
        weight = GC[:, 0:block, 0 : 3 * cols].reshape(dps * block, 3 * cols)
        y = jnp.dot(rows, weight, preferred_element_type=F32)
        Y[2 * i + 1 : 2 * i + 3] = y.reshape(2, pixels, 3 * cols)

    times = GC[:, block : block + 16, 0 : 3 * cols].reshape(dps * 16, 3 * cols)
    tb = jnp.dot(feat_ref[...], times, preferred_element_type=F32)
    bias = tb[0:1, 0:cols] + tb[1:2, cols : 2 * cols] + tb[2:3, 2 * cols : 3 * cols]

    def res_pair(p):
        both = []
        for i in (2 * p, 2 * p + 1):
            conv = Y[i][:, 0:cols] + Y[i + 1][:, cols : 2 * cols] + Y[i + 2][:, 2 * cols : 3 * cols]
            x = L[i].astype(F32)
            own = x[:, 0:cols]
            for j in range(1, planes):
                own = jnp.where(f == j, x[:, j * cols : (j + 1) * cols], own)
            both.append(own + (conv + bias))
        RS[f, p] = jnp.concatenate(both, axis=1).astype(BF16)

    def rs_copy(p, n):
        return remote(RS.at[f, p], RS.at[f, p], rs_s.at[p, n], rs_r.at[p, n], {"frame": side[n]})

    def rs_pass(p, n):
        part = pl.ds(n * (pixels // 2), pixels // 2)
        piece = RS.at[side[n], p, part]
        return remote(piece, piece, rs_s.at[p, 2 + n], rs_r.at[p, 2 + n], {"frame": side[1 - n]})

    def send_pair(p):
        res_pair(p)
        for n in range(2):
            rs_copy(p, n).start()

    def pass_pair(p):
        for n in range(2):
            rs_copy(p, n).wait_recv()
            rs_pass(p, n).start()

    conv_pair(0)
    for p in range(pairs):
        if p + 1 < pairs:
            conv_pair(p + 1)
        send_pair(p)

    def rows_of(p, n):
        return jnp.concatenate(
            [RS[j, p].astype(F32)[:, n * cols : (n + 1) * cols] for j in range(planes)], axis=1
        )

    def norm_pair(p):
        for n in range(2):
            rows = rows_of(p, n)
            mean = jnp.mean(rows, axis=-1, keepdims=True)
            dev = rows - mean
            var = jnp.mean(dev * dev, axis=-1, keepdims=True)
            H[2 * p + n] = (dev / jnp.sqrt(var + 1e-05)).astype(BF16)

    pad = jnp.zeros((pixels, HPAD - cols), F32)

    def triple_pair(i):
        rows = H[2 * i : 2 * i + 2].reshape(2 * pixels, channels)
        weight = GA[:, :, 0 : 3 * cols].reshape(dps * block, 3 * cols)
        y = jnp.dot(rows, weight, preferred_element_type=F32)
        for n in range(2):
            for t, buf in enumerate((Q, K, V)):
                piece = y[n * pixels : (n + 1) * pixels, t * cols : (t + 1) * cols]
                buf[2 * i + n] = jnp.concatenate([piece, pad], axis=1).astype(BF16)

    def arrive_pair(p):
        for n in range(2):
            rs_pass(p, n).wait_recv()
        norm_pair(p)

    waits = levels - 2
    for p in range(pairs):
        pass_pair(p)
        if p > 0:
            arrive_pair(p - 1)
        if p % 2 == 1 and p // 2 < waits:
            relay(1, 2 + p // 2)
    for step in range(2 + pairs // 2, levels):
        relay(1, step)
    from_sibling(1)

    half = dps * block // 2
    own_w = GA[:, :, 3 * cols : 4 * cols].reshape(dps * block, cols).astype(F32)
    WO[f] = jnp.concatenate([own_w[0:half], own_w[half : 2 * half]], axis=1).astype(BF16)
    quarter = half // 2
    wo_part = pl.ds(pl.multiple_of(c * quarter, 16), quarter)

    def wo_copy(j):
        piece = WO.at[f, wo_part]
        return remote(piece, piece, wo_s.at[j], wo_r.at[j, 0], {"frame": peer(j)})

    def wo_share(j):
        piece = WO.at[source(j), wo_part]
        return remote(piece, piece, wf_s.at[j], wo_r.at[j, 1], {"dp": sib})

    for j in range(1, planes):
        wo_copy(j).start()
    arrive_pair(pairs - 1)
    for p in range(pairs):
        triple_pair(p)

    def attend(p):
        prods = []
        for n in range(mine):
            q = Q[p * mine + n]
            prods.append(jnp.concatenate([q * K[g] for g in range(frames)], axis=1))
        prods = jnp.concatenate(prods, axis=0)
        scores = jnp.dot(prods, e_ref[...], preferred_element_type=F32) * (1.0 / math.sqrt(HD))
        peak = scores
        for shift in (8, 16, 32):
            peak = jnp.maximum(peak, pltpu.roll(peak, shift, 1))
        expo = jnp.exp(scores - peak)
        total = expo
        for shift in (8, 16, 32):
            total = total + pltpu.roll(total, shift, 1)
        probs = (expo / total).astype(BF16)
        acc = [0.0] * mine
        for g in range(frames):
            lanes = slice(g * HPAD, (g + 1) * HPAD)
            spreads = jnp.dot(probs, et_ref[:, lanes], preferred_element_type=F32)
            v = V[g].astype(F32)
            for n in range(mine):
                acc[n] = acc[n] + spreads[n * pixels : (n + 1) * pixels] * v
        return jnp.concatenate([part[:, 0:cols] for part in acc], axis=1)

    def attend_pair(j, carry):
        p = peer(j)
        ATS[p] = attend(p).astype(BF16)
        pl.when(j < planes)(lambda: at_copy(j).start())
        return carry

    def at_copy(j):
        p = peer(j)
        return remote(ATS.at[p], AT.at[f], at_s.at[j], at_r.at[j], {"frame": p})

    lax.fori_loop(1, planes + 1, attend_pair, 0)
    AT[f] = ATS[f]
    for j in range(1, planes):
        wo_copy(j).wait_recv()
        wo_share(j).start()
    for j in range(1, planes):
        wo_share(j).wait_recv()
    for j in range(1, planes):
        at_copy(j).wait_recv()

    wide = []
    for n in range(mine):
        heads = [AT[j].astype(F32)[:, n * cols : (n + 1) * cols] for j in range(planes)]
        wide.append(jnp.concatenate(heads, axis=1).astype(BF16))
    a = jnp.concatenate(wide, axis=0)
    parts = []
    for j in range(planes):
        left, right = WO[j][:, 0:cols], WO[j][:, cols : 2 * cols]
        part = jnp.dot(a[:, 0:half], left, preferred_element_type=F32)
        parts.append(part + jnp.dot(a[:, half : 2 * half], right, preferred_element_type=F32))
    mixed = jnp.concatenate(parts, axis=1)
    for n in range(mine):
        out_ref[n] = (rows_of(f, n) + mixed[n * pixels : (n + 1) * pixels]).astype(BF16)

    for j in range(1, planes):
        a_copy(0, j).wait_send()
        a_copy(1, j).wait_send()
        wo_copy(j).wait_send()
        wo_share(j).wait_send()
        at_copy(j).wait_send()
    for n in range(2):
        lat_copy(n).wait_send()
        lat_pass(n).wait_send()
        for p in range(pairs):
            rs_copy(p, n).wait_send()
            rs_pass(p, n).wait_send()
    drain(0)
    drain(1)


def indicators(frames, channels, cols):
    group = np.arange(channels) // (channels // GROUPS)
    ind = (group[:, None] == np.arange(128)[None, :]).astype(np.float32)
    row = np.arange(frames * HPAD)
    item, head = row // HPAD, (row % HPAD) // HD
    lane = np.arange(128)
    hit = (item[:, None] == (lane % 64)[None, :] // 8) & (head[:, None] == lane[None, :] % 8)
    hit = hit & (head < cols // HD)[:, None]
    back = (hit & (lane < 64)[None, :]).T
    return [jnp.asarray(m, BF16) for m in (ind, ind.T, hit.astype(np.float32), back.astype(np.float32))]


def fast_shards(latents, timestep, norm_gain, time_weight, conv_weight, attend_weight, output_weight):
    planes, dps = lax.axis_size("frame"), lax.axis_size("dp")
    _, mine, pixels, channels = latents.shape
    frames = mine * planes
    cols = channels // planes
    depth = conv_weight.shape[1]
    block = depth * planes
    f = lax.axis_index("frame")
    rows = time_weight.shape[0]
    features = sinusoid(timestep).astype(BF16).reshape(dps, rows)
    features = jnp.pad(features, ((0, 0), (0, 48 - rows))).reshape(dps, 3, 16)
    feats = jnp.pad(features.transpose(1, 0, 2).reshape(3, dps * 16), ((0, 13), (0, 0)))
    times = lax.dynamic_slice_in_dim(time_weight, f * cols, cols, axis=1)
    times = jnp.pad(times, ((0, 48 - rows), (0, 0))).reshape(3, 16, cols)
    times = times.transpose(1, 0, 2).reshape(16, 3 * cols)
    ind, indb, e, et = indicators(frames, channels, cols)
    vmem = pl.BlockSpec(memory_space=pltpu.VMEM)
    DMA = pltpu.SemaphoreType.DMA
    slots = 4 * (dps // 2)
    out = pl.pallas_call(
        functools.partial(kernel, planes, dps),
        out_shape=jax.ShapeDtypeStruct((mine, pixels, channels), BF16),
        in_specs=[vmem] * 11,
        out_specs=vmem,
        scratch_shapes=[
            pltpu.VMEM((frames, pixels, channels), BF16),
            pltpu.VMEM((frames, pixels, channels), BF16),
            pltpu.VMEM((planes, depth + 8, 3 * cols), BF16),
            pltpu.VMEM((planes, depth + 8, 4 * cols), BF16),
            pltpu.VMEM((planes, depth + 8, 3 * cols), BF16),
            pltpu.VMEM((planes, depth + 8, 4 * cols), BF16),
            pltpu.VMEM((dps, block + 16, 3 * cols), BF16),
            pltpu.VMEM((dps, block, 4 * cols), BF16),
            pltpu.VMEM((frames + 2, pixels, 3 * cols), F32),
            pltpu.VMEM((planes, frames // 2, pixels, 2 * cols), BF16),
            pltpu.VMEM((frames, pixels, HPAD), BF16),
            pltpu.VMEM((frames, pixels, HPAD), BF16),
            pltpu.VMEM((frames, pixels, HPAD), BF16),
            pltpu.VMEM((planes, pixels, 2 * cols), BF16),
            pltpu.VMEM((planes, pixels, 2 * cols), BF16),
            pltpu.VMEM((planes, dps * block // 2, 2 * cols), BF16),
            DMA((4,)), DMA((4,)),
            DMA((2, planes)), DMA((2, planes)),
            DMA((2, slots)), DMA((2, dps)),
            DMA((frames // 2, 4)), DMA((frames // 2, 4)),
            DMA((planes,)), DMA((planes,)),
            DMA((planes,)), DMA((planes, 2)), DMA((planes,)),
        ],
        compiler_params=pltpu.CompilerParams(
            collective_id=0, has_side_effects=True, vmem_limit_bytes=56 * 1024 * 1024
        ),
        cost_estimate=pl.CostEstimate(flops=7_000_000_000, bytes_accessed=8_000_000, transcendentals=3_000_000),
    )(
        latents[0], feats, norm_gain[None, :], times, conv_weight, attend_weight, output_weight,
        ind, indb, e, et,
    )
    return out[None]


def fits(mesh):
    planes, dps = mesh.shape["frame"], mesh.shape["dp"]
    return planes == 4 and dps == 8


def solution(mesh):
    in_specs = (
        P("dp", "frame", None, None),
        P("dp"),
        P(),
        P("dp", None),
        P(None, ("dp", "frame"), None),
        P(("dp", "frame"), None),
        P(("dp", "frame"), None),
    )
    out_specs = P("dp", "frame", None, None)
    return jax.shard_map(fast_shards if fits(mesh) else shards, mesh=mesh, in_specs=in_specs, out_specs=out_specs, check_vma=False)
```

```python
import functools
import math

import jax
import jax.numpy as jnp
import numpy as np
from jax import lax
from jax.experimental import pallas as pl
from jax.experimental.pallas import tpu as pltpu
from jax.sharding import PartitionSpec as P

HEADS = 20
HD = 64
GROUPS = 32
TEMB = 320


def with_halo(array, sides, width):
    for axis, dim in sides:
        count, length = (lax.axis_size(axis), array.shape[dim])
        up = [(i, (i + 1) % count) for i in range(count - 1)]
        down = [(j, i) for i, j in up]
        last = lax.slice_in_dim(array, length - width, length, axis=dim)
        initial = lax.slice_in_dim(array, 0, width, axis=dim)
        before = lax.ppermute(last, axis, up)
        after = lax.ppermute(initial, axis, down)
        array = jnp.concatenate([before, array, after], axis=dim)
    return array


def sinusoid(timestep):
    half_dim = TEMB // 2
    ladder = jnp.arange(half_dim, dtype=jnp.float32)
    freqs = jnp.exp(-math.log(10000.0) * ladder / half_dim)
    angles = timestep.astype(jnp.float32)[:, None] * freqs[None, :]
    return jnp.concatenate([jnp.cos(angles), jnp.sin(angles)], axis=-1)


def attend_pixels(triple):
    count_items, frames_all, pixels_here, width_three = triple.shape
    channels = width_three // 3
    parts = triple.reshape(count_items, frames_all, pixels_here, 3, HEADS, HD)
    queries = parts[:, :, :, 0]
    key_part = parts[:, :, :, 1]
    value_part = parts[:, :, :, 2]
    scores = jnp.einsum(
        "nfphd,ngphd->nphfg", queries, key_part, preferred_element_type=jnp.float32
    ) / math.sqrt(HD)
    peak = jnp.max(scores, axis=-1, keepdims=True)
    expo = jnp.exp(scores - peak)
    probs = (expo / jnp.sum(expo, axis=-1, keepdims=True)).astype(jnp.bfloat16)
    attended = jnp.einsum(
        "nphfg,ngphd->nfphd", probs, value_part, preferred_element_type=jnp.float32
    )
    attended = attended.astype(jnp.bfloat16).reshape(count_items, frames_all, pixels_here, channels)
    return lax.all_to_all(attended, "frame", split_axis=1, concat_axis=2, tiled=True)


def shards(latents, timestep, norm_gain, time_weight, conv_weight, attend_weight, output_weight):
    count_clips, frames_dev, pixels, channels = latents.shape
    group_width = channels // GROUPS
    time_full = lax.all_gather(time_weight, "dp", axis=0, tiled=True)
    features = sinusoid(timestep).astype(jnp.bfloat16)
    time_bias = jnp.dot(features, time_full, preferred_element_type=jnp.float32)
    conv_full, attend_full, output_full = (
        lax.all_gather(conv_weight, ("dp", "frame"), axis=1, tiled=True),
        lax.all_gather(attend_weight, ("dp", "frame"), axis=0, tiled=True),
        lax.all_gather(output_weight, ("dp", "frame"), axis=0, tiled=True),
    )
    values = latents.astype(jnp.float32)
    grouped = values.reshape(count_clips, frames_dev, pixels, GROUPS, group_width)
    members = frames_dev * lax.axis_size("frame") * pixels * group_width
    center = lax.psum(jnp.sum(grouped, axis=(1, 2, 4)), "frame") / members
    deviate = grouped - center[:, None, None, :, None]
    spread = lax.psum(jnp.sum(deviate * deviate, axis=(1, 2, 4)), "frame") / members
    normed_group = deviate / jnp.sqrt(spread[:, None, None, :, None] + 1e-05)
    scaled = normed_group.reshape(count_clips, frames_dev, pixels, channels) * norm_gain
    hidden = jax.nn.silu(scaled).astype(jnp.bfloat16)
    padded = with_halo(hidden, (("frame", 1),), 1)
    windows = [padded[:, offset : offset + frames_dev].reshape(-1, channels) for offset in range(3)]
    conv_init = jnp.zeros((count_clips * frames_dev * pixels, channels), jnp.float32)
    conv = conv_init
    for offset in range(3):
        conv = conv + jnp.dot(
            windows[offset], conv_full[offset], preferred_element_type=jnp.float32
        )
    conv = conv.reshape(count_clips, frames_dev, pixels, channels) + time_bias[:, None, None, :]
    residual = (values + conv).astype(jnp.bfloat16)
    rows = residual.astype(jnp.float32)
    row_mean = jnp.mean(rows, axis=-1, keepdims=True)
    row_var = jnp.mean((rows - row_mean) ** 2, axis=-1, keepdims=True)
    normed = ((rows - row_mean) / jnp.sqrt(row_var + 1e-05)).astype(jnp.bfloat16)
    product = jnp.dot(normed.reshape(-1, channels), attend_full, preferred_element_type=jnp.float32)
    triple = product.astype(jnp.bfloat16).reshape(count_clips, frames_dev, pixels, 3 * channels)
    attended = attend_pixels(
        lax.all_to_all(triple, "frame", split_axis=2, concat_axis=1, tiled=True)
    )
    flat_attended = attended.reshape(-1, channels)
    projected = jnp.dot(flat_attended, output_full, preferred_element_type=jnp.float32)
    mixed = rows + projected.reshape(count_clips, frames_dev, pixels, channels)
    return mixed.astype(jnp.bfloat16)


F32 = jnp.float32
BF16 = jnp.bfloat16
HPAD = 384


def split_rows(row):
    hi = row.astype(BF16).astype(F32)
    mid = (row - hi).astype(BF16).astype(F32)
    low = row - hi - mid
    place = lax.broadcasted_iota(jnp.int32, (16, row.shape[1]), 0)
    both = jnp.where(place == 0, hi, jnp.where(place == 1, mid, jnp.where(place == 2, low, 0.0)))
    return both.astype(BF16)


def group_mean(row, ind, ind_back, count):
    sums = jnp.dot(split_rows(row), ind, preferred_element_type=F32)
    sums = jnp.sum(sums, axis=0, keepdims=True) / count
    wide = jnp.dot(split_rows(sums), ind_back, preferred_element_type=F32)
    return jnp.sum(wide, axis=0, keepdims=True)


def kernel(
    planes, dps, lat_ref, step_ref, wave_ref, gain_ref, time_ref, conv_ref, att_ref, outw_ref,
    ind_ref, indb_ref, e_ref, et_ref, out_ref,
    L, H, S1, S2, A1, A2, GC, GA, Y, RS, Q, K, V, ATS, AT, WO,
    lat_s, lat_r, a_s, a_r, g_s, g_r, rs_s, rs_r, at_s, at_r, wo_s, wo_r, wf_s,
):
    d = lax.axis_index("dp")
    f = lax.axis_index("frame")
    z = d // 2
    c = d % 2
    sib = d + 1 - 2 * c
    levels = dps // 2
    frames, pixels, channels = L.shape
    mine = frames // planes
    cols = channels // planes
    depth = conv_ref.shape[1]
    block = planes * depth

    barrier = pltpu.get_barrier_semaphore()
    for j in range(1, planes):
        pl.semaphore_signal(barrier, inc=1, device_id={"frame": lax.rem(f + j, planes)}, device_id_type=pl.DeviceIdType.MESH)
    for j in range(1, dps):
        pl.semaphore_signal(barrier, inc=1, device_id={"dp": lax.rem(d + j, dps)}, device_id_type=pl.DeviceIdType.MESH)

    zeros3 = jnp.zeros((8, 3 * cols), F32)
    zeros4 = jnp.zeros((8, 4 * cols), F32)
    att = att_ref[...].astype(F32)
    outw = outw_ref[...].astype(F32)
    for j in range(planes):
        part = slice(j * cols, (j + 1) * cols)
        taps = [conv_ref[t].astype(F32)[:, part] for t in range(3)]
        S1[j] = jnp.concatenate([jnp.concatenate(taps, axis=1), zeros3], axis=0).astype(BF16)
        quads = [att[:, t * channels + j * cols : t * channels + (j + 1) * cols] for t in range(3)]
        quads.append(outw[:, part])
        S2[j] = jnp.concatenate([jnp.concatenate(quads, axis=1), zeros4], axis=0).astype(BF16)
    pl.semaphore_wait(barrier, planes - 1 + dps - 1)

    def remote(src, dst, ss, rs, where):
        return pltpu.make_async_remote_copy(
            src_ref=src, dst_ref=dst, send_sem=ss, recv_sem=rs, device_id=where,
            device_id_type=pl.DeviceIdType.MESH,
        )

    def peer(j):
        return lax.rem(f + j, planes)

    def source(j):
        return lax.rem(f + planes - j, planes)

    my_frames = pl.ds(f * mine, mine)

    def a_copy(k, j):
        src, dst = ((S1, A1), (S2, A2))[k]
        p = peer(j)
        return remote(src.at[p], dst.at[f], a_s.at[k, j], a_r.at[k, j], {"frame": p})

    side = [f + 1 - 2 * (f % 2), f + 2 - 4 * (f // 2)]
    diag = planes - 1 - f

    def lat_copy(n):
        return remote(lat_ref, L.at[my_frames], lat_s.at[n], lat_r.at[n], {"frame": side[n]})

    def lat_pass(n):
        part = pl.ds(side[n] * mine + n * (mine // 2), mine // 2)
        return remote(L.at[part], L.at[part], lat_s.at[2 + n], lat_r.at[2 + n], {"frame": side[1 - n]})

    for j in range(1, planes):
        a_copy(0, j).start()
    for n in range(2):
        lat_copy(n).start()
    for j in range(1, planes):
        a_copy(1, j).start()
    L[my_frames] = lat_ref[...]
    A1[f] = S1[f]
    A2[f] = S2[f]

    def stack(buf):
        return jnp.concatenate([buf[j].astype(F32)[:depth] for j in range(planes)], axis=0)

    G = (GC, GA)

    def g_copy(k, owner, slot, target):
        return remote(G[k].at[owner], G[k].at[owner], g_s.at[k, slot], g_r.at[k, owner], {"dp": target})

    def guarded(cond, fn):
        pl.when(cond)(fn)

    def steps_of(k, step, act):
        if step == 0:
            guarded(z < levels - 1, lambda: act(0, d, 0, d + 2))
            guarded(z > 0, lambda: act(0, d, 1, d - 2))
            act(0, d, 2, sib)
            return
        below = d - 2 * step
        above = d + 2 * step
        base = 4 * step - 1

        @pl.when(z >= step)
        def _():
            act(1, below, 0, sib)
            guarded(z < levels - 1, lambda: act(0, below, base, d + 2))
            act(0, below, base + 1, sib)

        @pl.when(z + step < levels)
        def _():
            act(1, above, 0, sib)
            guarded(z > 0, lambda: act(0, above, base + 2, d - 2))
            act(0, above, base + 3, sib)

    def relay(k, step):
        def act(kind, owner, slot, target):
            copy = g_copy(k, owner, slot, target)
            if kind == 1:
                copy.wait_recv()
            else:
                copy.start()

        steps_of(k, step, act)

    def drain(k):
        def act(kind, owner, slot, target):
            if kind == 0:
                g_copy(k, owner, slot, target).wait_send()

        for step in range(levels):
            steps_of(k, step, act)

    def from_sibling(k):
        for zz in range(levels):
            g_copy(k, 2 * zz + 1 - c, 0, sib).wait_recv()

    for j in range(1, planes):
        a_copy(0, j).wait_recv()
    GC[d, 0:block] = stack(A1).astype(BF16)
    times_all = time_ref[...].astype(F32)
    own_t = times_all[:, 0:cols]
    for j in range(1, planes):
        own_t = jnp.where(f == j, times_all[:, j * cols : (j + 1) * cols], own_t)
    own_t = jnp.concatenate([own_t, jnp.zeros((48 - own_t.shape[0], cols), F32)], axis=0)
    own_t = jnp.concatenate([own_t[16 * n : 16 * n + 16] for n in range(3)], axis=1)
    GC[d, block : block + 16] = own_t.astype(BF16)
    relay(0, 0)
    relay(0, 1)
    for n in range(2):
        lat_copy(n).wait_recv()
        lat_pass(n).start()
    for step in range(2, levels - 1):
        relay(0, step)
    for j in range(1, planes):
        a_copy(1, j).wait_recv()
    GA[d] = stack(A2).astype(BF16)
    relay(1, 0)

    for n in range(2):
        lat_pass(n).wait_recv()

    def fold(rows):
        return jnp.sum(rows.reshape(pixels // 8, 8, channels), axis=0)

    def sum_frame(i, acc):
        return acc + fold(L[i].astype(F32))

    start = jnp.zeros((8, channels), F32)
    total = lax.fori_loop(0, frames, sum_frame, start)
    count = float(frames * pixels * (channels // GROUPS))
    ind, indb = ind_ref[...], indb_ref[...]
    center = group_mean(jnp.sum(total, axis=0, keepdims=True), ind, indb, count)

    def dev_frame(i, acc):
        dev = L[i].astype(F32) - center
        return acc + fold(dev * dev)

    total2 = lax.fori_loop(0, frames, dev_frame, start)
    spread = group_mean(jnp.sum(total2, axis=0, keepdims=True), ind, indb, count)
    scale = gain_ref[...].reshape(1, channels) / jnp.sqrt(spread + 1e-05)

    def hide_frame(i, carry):
        scaled = (L[i].astype(F32) - center) * scale
        H[i] = (scaled / (1.0 + jnp.exp(-scaled))).astype(BF16)
        return carry

    relay(0, levels - 1)
    relay(1, 1)
    lax.fori_loop(0, frames, hide_frame, 0)

    from_sibling(0)
    Y[0] = jnp.zeros(Y.shape[1:], F32)
    Y[frames + 1] = jnp.zeros(Y.shape[1:], F32)

    pairs = frames // 2

    quad = 4

    def conv_quad(i):
        rows = H[quad * i : quad * (i + 1)].reshape(quad * pixels, channels)
        weight = GC[:, 0:block, 0 : 3 * cols].reshape(dps * block, 3 * cols)
        y = jnp.dot(rows, weight, preferred_element_type=F32)
        Y[quad * i + 1 : quad * (i + 1) + 1] = y.reshape(quad, pixels, 3 * cols)

    times = GC[:, block : block + 16, 0 : 3 * cols].reshape(dps * 16, 3 * cols)
    angles = step_ref[0].astype(F32) * wave_ref[0]
    which = wave_ref[1]
    feats = jnp.where(which == 1.0, jnp.cos(angles), jnp.where(which == 2.0, jnp.sin(angles), 0.0))
    tb = jnp.dot(feats.astype(BF16), times, preferred_element_type=F32)
    bias = tb[0:1, 0:cols] + tb[1:2, cols : 2 * cols] + tb[2:3, 2 * cols : 3 * cols]

    def res_pair(p):
        both = []
        for i in (2 * p, 2 * p + 1):
            conv = Y[i][:, 0:cols] + Y[i + 1][:, cols : 2 * cols] + Y[i + 2][:, 2 * cols : 3 * cols]
            x = L[i].astype(F32)
            own = x[:, 0:cols]
            for j in range(1, planes):
                own = jnp.where(f == j, x[:, j * cols : (j + 1) * cols], own)
            both.append(own + (conv + bias))
        RS[f, p] = jnp.concatenate(both, axis=1).astype(BF16)

    def rs_copy(p, n):
        return remote(RS.at[f, p], RS.at[f, p], rs_s.at[p, n], rs_r.at[p, n], {"frame": side[n]})

    def rs_pass(p, n):
        part = pl.ds(n * (pixels // 2), pixels // 2)
        piece = RS.at[side[n], p, part]
        return remote(piece, piece, rs_s.at[p, 2 + n], rs_r.at[p, 2 + n], {"frame": side[1 - n]})

    def send_pair(p):
        res_pair(p)
        for n in range(2):
            rs_copy(p, n).start()

    def pass_pair(p):
        for n in range(2):
            rs_copy(p, n).wait_recv()
            rs_pass(p, n).start()

    conv_quad(0)
    for p in range(pairs):
        if p % 2 == 1 and p + 1 < pairs:
            conv_quad((p + 1) // 2)
        send_pair(p)

    def rows_of(p, n):
        return jnp.concatenate(
            [RS[j, p].astype(F32)[:, n * cols : (n + 1) * cols] for j in range(planes)], axis=1
        )

    def norm_pair(p):
        for n in range(2):
            rows = rows_of(p, n)
            mean = jnp.mean(rows, axis=-1, keepdims=True)
            dev = rows - mean
            var = jnp.mean(dev * dev, axis=-1, keepdims=True)
            H[2 * p + n] = (dev / jnp.sqrt(var + 1e-05)).astype(BF16)

    pad = jnp.zeros((pixels, HPAD - cols), F32)

    def triple_quad(i):
        rows = H[quad * i : quad * (i + 1)].reshape(quad * pixels, channels)
        weight = GA[:, :, 0 : 3 * cols].reshape(dps * block, 3 * cols)
        y = jnp.dot(rows, weight, preferred_element_type=F32)
        for n in range(quad):
            for t, buf in enumerate((Q, K, V)):
                piece = y[n * pixels : (n + 1) * pixels, t * cols : (t + 1) * cols]
                buf[quad * i + n] = jnp.concatenate([piece, pad], axis=1).astype(BF16)

    def arrive_pair(p):
        for n in range(2):
            rs_pass(p, n).wait_recv()
        norm_pair(p)

    waits = levels - 2
    for p in range(pairs):
        pass_pair(p)
        if p > 0:
            arrive_pair(p - 1)
        if p % 2 == 1 and p // 2 < waits:
            relay(1, 2 + p // 2)
    for step in range(2 + pairs // 2, levels):
        relay(1, step)
    from_sibling(1)

    half = dps * block // 2
    own_w = GA[:, :, 3 * cols : 4 * cols].reshape(dps * block, cols).astype(F32)
    WO[f] = jnp.concatenate([own_w[0:half], own_w[half : 2 * half]], axis=1).astype(BF16)
    quarter = half // 2
    wo_part = pl.ds(pl.multiple_of(c * quarter, 16), quarter)

    def wo_copy(j):
        piece = WO.at[f, wo_part]
        return remote(piece, piece, wo_s.at[j], wo_r.at[j, 0], {"frame": peer(j)})

    def wo_share(j):
        piece = WO.at[source(j), wo_part]
        return remote(piece, piece, wf_s.at[j], wo_r.at[j, 1], {"dp": sib})

    for j in range(1, planes):
        wo_copy(j).start()
    arrive_pair(pairs - 1)
    for i in range(frames // quad):
        triple_quad(i)

    def attend(p):
        prods = []
        for n in range(mine):
            q = Q[p * mine + n]
            prods.append(jnp.concatenate([q * K[g] for g in range(frames)], axis=1))
        prods = jnp.concatenate(prods, axis=0)
        scores = jnp.dot(prods, e_ref[...], preferred_element_type=F32) * (1.0 / math.sqrt(HD))
        peak = scores
        for shift in (8, 16, 32):
            peak = jnp.maximum(peak, pltpu.roll(peak, shift, 1))
        expo = jnp.exp(scores - peak)
        total = expo
        for shift in (8, 16, 32):
            total = total + pltpu.roll(total, shift, 1)
        probs = (expo / total).astype(BF16)
        acc = [0.0] * mine
        for g in range(frames):
            lanes = slice(g * HPAD, (g + 1) * HPAD)
            spreads = jnp.dot(probs, et_ref[:, lanes], preferred_element_type=F32)
            v = V[g].astype(F32)
            for n in range(mine):
                acc[n] = acc[n] + spreads[n * pixels : (n + 1) * pixels] * v
        return jnp.concatenate([part[:, 0:cols] for part in acc], axis=1)

    def share_weight():
        for n in range(1, planes):
            wo_copy(n).wait_recv()
            wo_share(n).start()

    def attend_pair(j, carry):
        p = peer(j)
        pl.when(j == planes)(share_weight)
        ATS[p] = attend(p).astype(BF16)
        pl.when(j < planes)(lambda: at_copy(j).start())
        return carry

    def at_copy(j):
        p = peer(j)
        return remote(ATS.at[p], AT.at[f], at_s.at[j], at_r.at[j], {"frame": p})

    lax.fori_loop(1, planes + 1, attend_pair, 0)
    AT[f] = ATS[f]
    for j in range(1, planes):
        wo_share(j).wait_recv()
    for j in range(1, planes):
        at_copy(j).wait_recv()

    wide = []
    for n in range(mine):
        heads = [AT[j].astype(F32)[:, n * cols : (n + 1) * cols] for j in range(planes)]
        wide.append(jnp.concatenate(heads, axis=1).astype(BF16))
    a = jnp.concatenate(wide, axis=0)
    parts = []
    for j in range(planes):
        left, right = WO[j][:, 0:cols], WO[j][:, cols : 2 * cols]
        part = jnp.dot(a[:, 0:half], left, preferred_element_type=F32)
        parts.append(part + jnp.dot(a[:, half : 2 * half], right, preferred_element_type=F32))
    mixed = jnp.concatenate(parts, axis=1)
    for n in range(mine):
        out_ref[n] = (rows_of(f, n) + mixed[n * pixels : (n + 1) * pixels]).astype(BF16)

    for j in range(1, planes):
        a_copy(0, j).wait_send()
        a_copy(1, j).wait_send()
        wo_copy(j).wait_send()
        wo_share(j).wait_send()
        at_copy(j).wait_send()
    for n in range(2):
        lat_copy(n).wait_send()
        lat_pass(n).wait_send()
        for p in range(pairs):
            rs_copy(p, n).wait_send()
            rs_pass(p, n).wait_send()
    drain(0)
    drain(1)


def indicators(frames, channels, cols):
    group = np.arange(channels) // (channels // GROUPS)
    ind = (group[:, None] == np.arange(128)[None, :]).astype(np.float32)
    row = np.arange(frames * HPAD)
    item, head = row // HPAD, (row % HPAD) // HD
    lane = np.arange(128)
    hit = (item[:, None] == (lane % 64)[None, :] // 8) & (head[:, None] == lane[None, :] % 8)
    hit = hit & (head < cols // HD)[:, None]
    back = (hit & (lane < 64)[None, :]).T
    return [jnp.asarray(m, BF16) for m in (ind, ind.T, hit.astype(np.float32), back.astype(np.float32))]


def fast_shards(latents, timestep, norm_gain, time_weight, conv_weight, attend_weight, output_weight):
    planes, dps = lax.axis_size("frame"), lax.axis_size("dp")
    _, mine, pixels, channels = latents.shape
    frames = mine * planes
    cols = channels // planes
    depth = conv_weight.shape[1]
    block = depth * planes
    rows = time_weight.shape[0]
    lane, line = np.arange(dps * 16)[None, :], np.arange(16)[:, None]
    inside = 16 * line + lane % 16
    entry = rows * (lane // 16) + inside
    half_dim = TEMB // 2
    ladder = (entry % half_dim).astype(np.float32)
    freqs = np.exp(np.float32(-math.log(10000.0)) * ladder / np.float32(half_dim))
    which = np.where(inside < rows, 1.0 + (entry >= half_dim), 0.0)
    wave = jnp.asarray(np.stack([freqs, which]), F32)
    ind, indb, e, et = indicators(frames, channels, cols)
    vmem = pl.BlockSpec(memory_space=pltpu.VMEM)
    DMA = pltpu.SemaphoreType.DMA
    slots = 4 * (dps // 2)
    out = pl.pallas_call(
        functools.partial(kernel, planes, dps),
        out_shape=jax.ShapeDtypeStruct((mine, pixels, channels), BF16),
        in_specs=[vmem, pl.BlockSpec(memory_space=pltpu.SMEM)] + [vmem] * 10,
        out_specs=vmem,
        scratch_shapes=[
            pltpu.VMEM((frames, pixels, channels), BF16),
            pltpu.VMEM((frames, pixels, channels), BF16),
            pltpu.VMEM((planes, depth + 8, 3 * cols), BF16),
            pltpu.VMEM((planes, depth + 8, 4 * cols), BF16),
            pltpu.VMEM((planes, depth + 8, 3 * cols), BF16),
            pltpu.VMEM((planes, depth + 8, 4 * cols), BF16),
            pltpu.VMEM((dps, block + 16, 3 * cols), BF16),
            pltpu.VMEM((dps, block, 4 * cols), BF16),
            pltpu.VMEM((frames + 2, pixels, 3 * cols), F32),
            pltpu.VMEM((planes, frames // 2, pixels, 2 * cols), BF16),
            pltpu.VMEM((frames, pixels, HPAD), BF16),
            pltpu.VMEM((frames, pixels, HPAD), BF16),
            pltpu.VMEM((frames, pixels, HPAD), BF16),
            pltpu.VMEM((planes, pixels, 2 * cols), BF16),
            pltpu.VMEM((planes, pixels, 2 * cols), BF16),
            pltpu.VMEM((planes, dps * block // 2, 2 * cols), BF16),
            DMA((4,)), DMA((4,)),
            DMA((2, planes)), DMA((2, planes)),
            DMA((2, slots)), DMA((2, dps)),
            DMA((frames // 2, 4)), DMA((frames // 2, 4)),
            DMA((planes,)), DMA((planes,)),
            DMA((planes,)), DMA((planes, 2)), DMA((planes,)),
        ],
        compiler_params=pltpu.CompilerParams(
            collective_id=0, has_side_effects=True, vmem_limit_bytes=56 * 1024 * 1024
        ),
        cost_estimate=pl.CostEstimate(flops=7_000_000_000, bytes_accessed=8_000_000, transcendentals=3_000_000),
    )(
        latents[0], timestep, wave, norm_gain, time_weight, conv_weight, attend_weight, output_weight,
        ind, indb, e, et,
    )
    return out[None]


def fits(mesh):
    planes, dps = mesh.shape["frame"], mesh.shape["dp"]
    return planes == 4 and dps == 8


def solution(mesh):
    in_specs = (
        P("dp", "frame", None, None),
        P("dp"),
        P(),
        P("dp", None),
        P(None, ("dp", "frame"), None),
        P(("dp", "frame"), None),
        P(("dp", "frame"), None),
    )
    out_specs = P("dp", "frame", None, None)
    return jax.shard_map(fast_shards if fits(mesh) else shards, mesh=mesh, in_specs=in_specs, out_specs=out_specs, check_vma=False)
```

```python
import functools
import math

import jax
import jax.numpy as jnp
import numpy as np
from jax import lax
from jax.experimental import pallas as pl
from jax.experimental.pallas import tpu as pltpu
from jax.sharding import PartitionSpec as P

HEADS = 20
HD = 64
GROUPS = 32
TEMB = 320


def with_halo(array, sides, width):
    for axis, dim in sides:
        count, length = (lax.axis_size(axis), array.shape[dim])
        up = [(i, (i + 1) % count) for i in range(count - 1)]
        down = [(j, i) for i, j in up]
        last = lax.slice_in_dim(array, length - width, length, axis=dim)
        initial = lax.slice_in_dim(array, 0, width, axis=dim)
        before = lax.ppermute(last, axis, up)
        after = lax.ppermute(initial, axis, down)
        array = jnp.concatenate([before, array, after], axis=dim)
    return array


def sinusoid(timestep):
    half_dim = TEMB // 2
    ladder = jnp.arange(half_dim, dtype=jnp.float32)
    freqs = jnp.exp(-math.log(10000.0) * ladder / half_dim)
    angles = timestep.astype(jnp.float32)[:, None] * freqs[None, :]
    return jnp.concatenate([jnp.cos(angles), jnp.sin(angles)], axis=-1)


def attend_pixels(triple):
    count_items, frames_all, pixels_here, width_three = triple.shape
    channels = width_three // 3
    parts = triple.reshape(count_items, frames_all, pixels_here, 3, HEADS, HD)
    queries = parts[:, :, :, 0]
    key_part = parts[:, :, :, 1]
    value_part = parts[:, :, :, 2]
    scores = jnp.einsum(
        "nfphd,ngphd->nphfg", queries, key_part, preferred_element_type=jnp.float32
    ) / math.sqrt(HD)
    peak = jnp.max(scores, axis=-1, keepdims=True)
    expo = jnp.exp(scores - peak)
    probs = (expo / jnp.sum(expo, axis=-1, keepdims=True)).astype(jnp.bfloat16)
    attended = jnp.einsum(
        "nphfg,ngphd->nfphd", probs, value_part, preferred_element_type=jnp.float32
    )
    attended = attended.astype(jnp.bfloat16).reshape(count_items, frames_all, pixels_here, channels)
    return lax.all_to_all(attended, "frame", split_axis=1, concat_axis=2, tiled=True)


def shards(latents, timestep, norm_gain, time_weight, conv_weight, attend_weight, output_weight):
    count_clips, frames_dev, pixels, channels = latents.shape
    group_width = channels // GROUPS
    time_full = lax.all_gather(time_weight, "dp", axis=0, tiled=True)
    features = sinusoid(timestep).astype(jnp.bfloat16)
    time_bias = jnp.dot(features, time_full, preferred_element_type=jnp.float32)
    conv_full, attend_full, output_full = (
        lax.all_gather(conv_weight, ("dp", "frame"), axis=1, tiled=True),
        lax.all_gather(attend_weight, ("dp", "frame"), axis=0, tiled=True),
        lax.all_gather(output_weight, ("dp", "frame"), axis=0, tiled=True),
    )
    values = latents.astype(jnp.float32)
    grouped = values.reshape(count_clips, frames_dev, pixels, GROUPS, group_width)
    members = frames_dev * lax.axis_size("frame") * pixels * group_width
    center = lax.psum(jnp.sum(grouped, axis=(1, 2, 4)), "frame") / members
    deviate = grouped - center[:, None, None, :, None]
    spread = lax.psum(jnp.sum(deviate * deviate, axis=(1, 2, 4)), "frame") / members
    normed_group = deviate / jnp.sqrt(spread[:, None, None, :, None] + 1e-05)
    scaled = normed_group.reshape(count_clips, frames_dev, pixels, channels) * norm_gain
    hidden = jax.nn.silu(scaled).astype(jnp.bfloat16)
    padded = with_halo(hidden, (("frame", 1),), 1)
    windows = [padded[:, offset : offset + frames_dev].reshape(-1, channels) for offset in range(3)]
    conv_init = jnp.zeros((count_clips * frames_dev * pixels, channels), jnp.float32)
    conv = conv_init
    for offset in range(3):
        conv = conv + jnp.dot(
            windows[offset], conv_full[offset], preferred_element_type=jnp.float32
        )
    conv = conv.reshape(count_clips, frames_dev, pixels, channels) + time_bias[:, None, None, :]
    residual = (values + conv).astype(jnp.bfloat16)
    rows = residual.astype(jnp.float32)
    row_mean = jnp.mean(rows, axis=-1, keepdims=True)
    row_var = jnp.mean((rows - row_mean) ** 2, axis=-1, keepdims=True)
    normed = ((rows - row_mean) / jnp.sqrt(row_var + 1e-05)).astype(jnp.bfloat16)
    product = jnp.dot(normed.reshape(-1, channels), attend_full, preferred_element_type=jnp.float32)
    triple = product.astype(jnp.bfloat16).reshape(count_clips, frames_dev, pixels, 3 * channels)
    attended = attend_pixels(
        lax.all_to_all(triple, "frame", split_axis=2, concat_axis=1, tiled=True)
    )
    flat_attended = attended.reshape(-1, channels)
    projected = jnp.dot(flat_attended, output_full, preferred_element_type=jnp.float32)
    mixed = rows + projected.reshape(count_clips, frames_dev, pixels, channels)
    return mixed.astype(jnp.bfloat16)


F32 = jnp.float32
BF16 = jnp.bfloat16
HPAD = 384


def split_rows(row):
    hi = row.astype(BF16).astype(F32)
    mid = (row - hi).astype(BF16).astype(F32)
    low = row - hi - mid
    place = lax.broadcasted_iota(jnp.int32, (16, row.shape[1]), 0)
    both = jnp.where(place == 0, hi, jnp.where(place == 1, mid, jnp.where(place == 2, low, 0.0)))
    return both.astype(BF16)


def group_mean(row, ind, ind_back, count):
    sums = jnp.dot(split_rows(row), ind, preferred_element_type=F32)
    sums = jnp.sum(sums, axis=0, keepdims=True) / count
    wide = jnp.dot(split_rows(sums), ind_back, preferred_element_type=F32)
    return jnp.sum(wide, axis=0, keepdims=True)


def kernel(
    planes, dps, lat_ref, step_ref, wave_ref, gain_ref, time_ref, conv_ref, att_ref, outw_ref,
    ind_ref, indb_ref, e_ref, et_ref, out_ref,
    L, H, S1, S2, A1, A2, GC, GA, Y, RS, Q, K, V, ATS, AT, WO,
    lat_s, lat_r, a_s, a_r, g_s, g_r, rs_s, rs_r, at_s, at_r, wo_s, wo_r, wf_s,
):
    d = lax.axis_index("dp")
    f = lax.axis_index("frame")
    z = d // 2
    c = d % 2
    sib = d + 1 - 2 * c
    levels = dps // 2
    frames, pixels, channels = L.shape
    mine = frames // planes
    cols = channels // planes
    depth = conv_ref.shape[1]
    block = planes * depth

    barrier = pltpu.get_barrier_semaphore()
    for j in range(1, planes):
        pl.semaphore_signal(barrier, inc=1, device_id={"frame": lax.rem(f + j, planes)}, device_id_type=pl.DeviceIdType.MESH)
    for j in range(1, dps):
        pl.semaphore_signal(barrier, inc=1, device_id={"dp": lax.rem(d + j, dps)}, device_id_type=pl.DeviceIdType.MESH)

    zeros3 = jnp.zeros((8, 3 * cols), F32)
    zeros4 = jnp.zeros((8, 4 * cols), F32)
    att = att_ref[...].astype(F32)
    outw = outw_ref[...].astype(F32)
    for j in range(planes):
        part = slice(j * cols, (j + 1) * cols)
        taps = [conv_ref[t].astype(F32)[:, part] for t in range(3)]
        S1[j] = jnp.concatenate([jnp.concatenate(taps, axis=1), zeros3], axis=0).astype(BF16)
        quads = [att[:, t * channels + j * cols : t * channels + (j + 1) * cols] for t in range(3)]
        quads.append(outw[:, part])
        S2[j] = jnp.concatenate([jnp.concatenate(quads, axis=1), zeros4], axis=0).astype(BF16)
    pl.semaphore_wait(barrier, planes - 1 + dps - 1)

    def remote(src, dst, ss, rs, where):
        return pltpu.make_async_remote_copy(
            src_ref=src, dst_ref=dst, send_sem=ss, recv_sem=rs, device_id=where,
            device_id_type=pl.DeviceIdType.MESH,
        )

    def peer(j):
        return lax.rem(f + j, planes)

    def source(j):
        return lax.rem(f + planes - j, planes)

    my_frames = pl.ds(f * mine, mine)

    def a_copy(k, j):
        src, dst = ((S1, A1), (S2, A2))[k]
        p = peer(j)
        return remote(src.at[p], dst.at[f], a_s.at[k, j], a_r.at[k, j], {"frame": p})

    side = [f + 1 - 2 * (f % 2), f + 2 - 4 * (f // 2)]
    diag = planes - 1 - f

    def lat_copy(n):
        return remote(lat_ref, L.at[my_frames], lat_s.at[n], lat_r.at[n], {"frame": side[n]})

    def lat_pass(n):
        part = pl.ds(side[n] * mine + n * (mine // 2), mine // 2)
        return remote(L.at[part], L.at[part], lat_s.at[2 + n], lat_r.at[2 + n], {"frame": side[1 - n]})

    for j in range(1, planes):
        a_copy(0, j).start()
    for n in range(2):
        lat_copy(n).start()
    for j in range(1, planes):
        a_copy(1, j).start()
    L[my_frames] = lat_ref[...]
    A1[f] = S1[f]
    A2[f] = S2[f]

    def stack(buf):
        return jnp.concatenate([buf[j].astype(F32)[:depth] for j in range(planes)], axis=0)

    cut = block // 2
    G = ((GC, 0, cut), (GC, cut, cut + 16), (GA, 0, cut), (GA, cut, cut))

    def g_copy(k, owner, slot, target):
        buf, first, size = G[k]
        piece = buf.at[owner, pl.ds(first, size)]
        return remote(piece, piece, g_s.at[k, slot], g_r.at[k, owner], {"dp": target})

    def guarded(cond, fn):
        pl.when(cond)(fn)

    def steps_of(k, step, act):
        if step == 0:
            guarded(z < levels - 1, lambda: act(0, d, 0, d + 2))
            guarded(z > 0, lambda: act(0, d, 1, d - 2))
            act(0, d, 2, sib)
            return
        below = d - 2 * step
        above = d + 2 * step
        base = 4 * step - 1

        @pl.when(z >= step)
        def _():
            act(1, below, 0, sib)
            guarded(z < levels - 1, lambda: act(0, below, base, d + 2))
            act(0, below, base + 1, sib)

        @pl.when(z + step < levels)
        def _():
            act(1, above, 0, sib)
            guarded(z > 0, lambda: act(0, above, base + 2, d - 2))
            act(0, above, base + 3, sib)

    def relay(which, step):
        relay_half(2 * which, step)
        relay_half(2 * which + 1, step)

    def relay_half(k, step):
        def act(kind, owner, slot, target):
            copy = g_copy(k, owner, slot, target)
            if kind == 1:
                copy.wait_recv()
            else:
                copy.start()

        steps_of(k, step, act)

    def drain(k):
        def act(kind, owner, slot, target):
            if kind == 0:
                g_copy(k, owner, slot, target).wait_send()

        for step in range(levels):
            steps_of(k, step, act)

    def from_sibling(which):
        for k in (2 * which, 2 * which + 1):
            for zz in range(levels):
                g_copy(k, 2 * zz + 1 - c, 0, sib).wait_recv()

    for j in range(1, planes):
        a_copy(0, j).wait_recv()
    GC[d, 0:block] = stack(A1).astype(BF16)
    times_all = time_ref[...].astype(F32)
    own_t = times_all[:, 0:cols]
    for j in range(1, planes):
        own_t = jnp.where(f == j, times_all[:, j * cols : (j + 1) * cols], own_t)
    own_t = jnp.concatenate([own_t, jnp.zeros((48 - own_t.shape[0], cols), F32)], axis=0)
    own_t = jnp.concatenate([own_t[16 * n : 16 * n + 16] for n in range(3)], axis=1)
    GC[d, block : block + 16] = own_t.astype(BF16)
    relay(0, 0)
    relay(0, 1)
    for n in range(2):
        lat_copy(n).wait_recv()
        lat_pass(n).start()
    for step in range(2, levels - 1):
        relay(0, step)
    for j in range(1, planes):
        a_copy(1, j).wait_recv()
    GA[d] = stack(A2).astype(BF16)
    relay(1, 0)

    for n in range(2):
        lat_pass(n).wait_recv()

    def fold(rows):
        return jnp.sum(rows.reshape(pixels // 8, 8, channels), axis=0)

    def sum_frame(i, acc):
        return acc + fold(L[i].astype(F32))

    start = jnp.zeros((8, channels), F32)
    total = lax.fori_loop(0, frames, sum_frame, start)
    count = float(frames * pixels * (channels // GROUPS))
    ind, indb = ind_ref[...], indb_ref[...]
    center = group_mean(jnp.sum(total, axis=0, keepdims=True), ind, indb, count)

    def dev_frame(i, acc):
        dev = L[i].astype(F32) - center
        return acc + fold(dev * dev)

    total2 = lax.fori_loop(0, frames, dev_frame, start)
    spread = group_mean(jnp.sum(total2, axis=0, keepdims=True), ind, indb, count)
    scale = gain_ref[...].reshape(1, channels) / jnp.sqrt(spread + 1e-05)

    def hide_frame(i, carry):
        scaled = (L[i].astype(F32) - center) * scale
        H[i] = (scaled / (1.0 + jnp.exp(-scaled))).astype(BF16)
        return carry

    relay(0, levels - 1)
    relay(1, 1)
    lax.fori_loop(0, frames, hide_frame, 0)

    from_sibling(0)
    Y[0] = jnp.zeros(Y.shape[1:], F32)
    Y[frames + 1] = jnp.zeros(Y.shape[1:], F32)

    pairs = frames // 2

    quad = 4

    def conv_quad(i):
        rows = H[quad * i : quad * (i + 1)].reshape(quad * pixels, channels)
        weight = GC[:, 0:block, 0 : 3 * cols].reshape(dps * block, 3 * cols)
        y = jnp.dot(rows, weight, preferred_element_type=F32)
        Y[quad * i + 1 : quad * (i + 1) + 1] = y.reshape(quad, pixels, 3 * cols)

    times = GC[:, block : block + 16, 0 : 3 * cols].reshape(dps * 16, 3 * cols)
    angles = step_ref[0].astype(F32) * wave_ref[0]
    which = wave_ref[1]
    feats = jnp.where(which == 1.0, jnp.cos(angles), jnp.where(which == 2.0, jnp.sin(angles), 0.0))
    tb = jnp.dot(feats.astype(BF16), times, preferred_element_type=F32)
    bias = tb[0:1, 0:cols] + tb[1:2, cols : 2 * cols] + tb[2:3, 2 * cols : 3 * cols]

    def res_pair(p):
        both = []
        for i in (2 * p, 2 * p + 1):
            conv = Y[i][:, 0:cols] + Y[i + 1][:, cols : 2 * cols] + Y[i + 2][:, 2 * cols : 3 * cols]
            x = L[i].astype(F32)
            own = x[:, 0:cols]
            for j in range(1, planes):
                own = jnp.where(f == j, x[:, j * cols : (j + 1) * cols], own)
            both.append(own + (conv + bias))
        RS[f, p] = jnp.concatenate(both, axis=1).astype(BF16)

    def rs_copy(p, n):
        return remote(RS.at[f, p], RS.at[f, p], rs_s.at[p, n], rs_r.at[p, n], {"frame": side[n]})

    def rs_pass(p, n):
        part = pl.ds(n * (pixels // 2), pixels // 2)
        piece = RS.at[side[n], p, part]
        return remote(piece, piece, rs_s.at[p, 2 + n], rs_r.at[p, 2 + n], {"frame": side[1 - n]})

    def send_pair(p):
        res_pair(p)
        for n in range(2):
            rs_copy(p, n).start()

    def pass_pair(p):
        for n in range(2):
            rs_copy(p, n).wait_recv()
            rs_pass(p, n).start()

    conv_quad(0)
    for p in range(pairs):
        if p % 2 == 1 and p + 1 < pairs:
            conv_quad((p + 1) // 2)
        send_pair(p)

    def rows_of(p, n):
        return jnp.concatenate(
            [RS[j, p].astype(F32)[:, n * cols : (n + 1) * cols] for j in range(planes)], axis=1
        )

    def norm_pair(p):
        for n in range(2):
            rows = rows_of(p, n)
            mean = jnp.mean(rows, axis=-1, keepdims=True)
            dev = rows - mean
            var = jnp.mean(dev * dev, axis=-1, keepdims=True)
            H[2 * p + n] = (dev / jnp.sqrt(var + 1e-05)).astype(BF16)

    pad = jnp.zeros((pixels, HPAD - cols), F32)

    def triple_quad(i):
        rows = H[quad * i : quad * (i + 1)].reshape(quad * pixels, channels)
        weight = GA[:, :, 0 : 3 * cols].reshape(dps * block, 3 * cols)
        y = jnp.dot(rows, weight, preferred_element_type=F32)
        for n in range(quad):
            for t, buf in enumerate((Q, K, V)):
                piece = y[n * pixels : (n + 1) * pixels, t * cols : (t + 1) * cols]
                buf[quad * i + n] = jnp.concatenate([piece, pad], axis=1).astype(BF16)

    def arrive_pair(p):
        for n in range(2):
            rs_pass(p, n).wait_recv()
        norm_pair(p)

    waits = levels - 2
    for p in range(pairs):
        pass_pair(p)
        if p > 0:
            arrive_pair(p - 1)
        if p % 2 == 1 and p // 2 < waits:
            relay(1, 2 + p // 2)
    for step in range(2 + pairs // 2, levels):
        relay(1, step)
    from_sibling(1)

    half = dps * block // 2
    own_w = GA[:, :, 3 * cols : 4 * cols].reshape(dps * block, cols).astype(F32)
    WO[f] = jnp.concatenate([own_w[0:half], own_w[half : 2 * half]], axis=1).astype(BF16)
    quarter = half // 2
    wo_part = pl.ds(pl.multiple_of(c * quarter, 16), quarter)

    def wo_copy(j):
        piece = WO.at[f, wo_part]
        return remote(piece, piece, wo_s.at[j], wo_r.at[j, 0], {"frame": peer(j)})

    def wo_share(j):
        piece = WO.at[source(j), wo_part]
        return remote(piece, piece, wf_s.at[j], wo_r.at[j, 1], {"dp": sib})

    for j in range(1, planes):
        wo_copy(j).start()
    arrive_pair(pairs - 1)
    for i in range(frames // quad):
        triple_quad(i)

    def attend(p):
        prods = []
        for n in range(mine):
            q = Q[p * mine + n]
            prods.append(jnp.concatenate([q * K[g] for g in range(frames)], axis=1))
        prods = jnp.concatenate(prods, axis=0)
        scores = jnp.dot(prods, e_ref[...], preferred_element_type=F32) * (1.0 / math.sqrt(HD))
        peak = scores
        for shift in (8, 16, 32):
            peak = jnp.maximum(peak, pltpu.roll(peak, shift, 1))
        expo = jnp.exp(scores - peak)
        total = expo
        for shift in (8, 16, 32):
            total = total + pltpu.roll(total, shift, 1)
        probs = (expo / total).astype(BF16)
        acc = [0.0] * mine
        for g in range(frames):
            lanes = slice(g * HPAD, (g + 1) * HPAD)
            spreads = jnp.dot(probs, et_ref[:, lanes], preferred_element_type=F32)
            v = V[g].astype(F32)
            for n in range(mine):
                acc[n] = acc[n] + spreads[n * pixels : (n + 1) * pixels] * v
        return jnp.concatenate([part[:, 0:cols] for part in acc], axis=1)

    def share_weight():
        for n in range(1, planes):
            wo_copy(n).wait_recv()
            wo_share(n).start()

    def attend_pair(j, carry):
        p = peer(j)
        pl.when(j == planes)(share_weight)
        ATS[p] = attend(p).astype(BF16)
        pl.when(j < planes)(lambda: at_copy(j).start())
        return carry

    def at_copy(j):
        p = peer(j)
        return remote(ATS.at[p], AT.at[f], at_s.at[j], at_r.at[j], {"frame": p})

    lax.fori_loop(1, planes + 1, attend_pair, 0)
    AT[f] = ATS[f]
    for j in range(1, planes):
        wo_share(j).wait_recv()
    for j in range(1, planes):
        at_copy(j).wait_recv()

    wide = []
    for n in range(mine):
        heads = [AT[j].astype(F32)[:, n * cols : (n + 1) * cols] for j in range(planes)]
        wide.append(jnp.concatenate(heads, axis=1).astype(BF16))
    a = jnp.concatenate(wide, axis=0)
    parts = []
    for j in range(planes):
        left, right = WO[j][:, 0:cols], WO[j][:, cols : 2 * cols]
        part = jnp.dot(a[:, 0:half], left, preferred_element_type=F32)
        parts.append(part + jnp.dot(a[:, half : 2 * half], right, preferred_element_type=F32))
    mixed = jnp.concatenate(parts, axis=1)
    for n in range(mine):
        out_ref[n] = (rows_of(f, n) + mixed[n * pixels : (n + 1) * pixels]).astype(BF16)

    for j in range(1, planes):
        a_copy(0, j).wait_send()
        a_copy(1, j).wait_send()
        wo_copy(j).wait_send()
        wo_share(j).wait_send()
        at_copy(j).wait_send()
    for n in range(2):
        lat_copy(n).wait_send()
        lat_pass(n).wait_send()
        for p in range(pairs):
            rs_copy(p, n).wait_send()
            rs_pass(p, n).wait_send()
    for k in range(4):
        drain(k)


def indicators(frames, channels, cols):
    group = np.arange(channels) // (channels // GROUPS)
    ind = (group[:, None] == np.arange(128)[None, :]).astype(np.float32)
    row = np.arange(frames * HPAD)
    item, head = row // HPAD, (row % HPAD) // HD
    lane = np.arange(128)
    hit = (item[:, None] == (lane % 64)[None, :] // 8) & (head[:, None] == lane[None, :] % 8)
    hit = hit & (head < cols // HD)[:, None]
    back = (hit & (lane < 64)[None, :]).T
    return [jnp.asarray(m, BF16) for m in (ind, ind.T, hit.astype(np.float32), back.astype(np.float32))]


def fast_shards(latents, timestep, norm_gain, time_weight, conv_weight, attend_weight, output_weight):
    planes, dps = lax.axis_size("frame"), lax.axis_size("dp")
    _, mine, pixels, channels = latents.shape
    frames = mine * planes
    cols = channels // planes
    depth = conv_weight.shape[1]
    block = depth * planes
    rows = time_weight.shape[0]
    lane, line = np.arange(dps * 16)[None, :], np.arange(16)[:, None]
    inside = 16 * line + lane % 16
    entry = rows * (lane // 16) + inside
    half_dim = TEMB // 2
    ladder = (entry % half_dim).astype(np.float32)
    freqs = np.exp(np.float32(-math.log(10000.0)) * ladder / np.float32(half_dim))
    which = np.where(inside < rows, 1.0 + (entry >= half_dim), 0.0)
    wave = jnp.asarray(np.stack([freqs, which]), F32)
    ind, indb, e, et = indicators(frames, channels, cols)
    vmem = pl.BlockSpec(memory_space=pltpu.VMEM)
    DMA = pltpu.SemaphoreType.DMA
    slots = 4 * (dps // 2)
    out = pl.pallas_call(
        functools.partial(kernel, planes, dps),
        out_shape=jax.ShapeDtypeStruct((mine, pixels, channels), BF16),
        in_specs=[vmem, pl.BlockSpec(memory_space=pltpu.SMEM)] + [vmem] * 10,
        out_specs=vmem,
        scratch_shapes=[
            pltpu.VMEM((frames, pixels, channels), BF16),
            pltpu.VMEM((frames, pixels, channels), BF16),
            pltpu.VMEM((planes, depth + 8, 3 * cols), BF16),
            pltpu.VMEM((planes, depth + 8, 4 * cols), BF16),
            pltpu.VMEM((planes, depth + 8, 3 * cols), BF16),
            pltpu.VMEM((planes, depth + 8, 4 * cols), BF16),
            pltpu.VMEM((dps, block + 16, 3 * cols), BF16),
            pltpu.VMEM((dps, block, 4 * cols), BF16),
            pltpu.VMEM((frames + 2, pixels, 3 * cols), F32),
            pltpu.VMEM((planes, frames // 2, pixels, 2 * cols), BF16),
            pltpu.VMEM((frames, pixels, HPAD), BF16),
            pltpu.VMEM((frames, pixels, HPAD), BF16),
            pltpu.VMEM((frames, pixels, HPAD), BF16),
            pltpu.VMEM((planes, pixels, 2 * cols), BF16),
            pltpu.VMEM((planes, pixels, 2 * cols), BF16),
            pltpu.VMEM((planes, dps * block // 2, 2 * cols), BF16),
            DMA((4,)), DMA((4,)),
            DMA((2, planes)), DMA((2, planes)),
            DMA((4, slots)), DMA((4, dps)),
            DMA((frames // 2, 4)), DMA((frames // 2, 4)),
            DMA((planes,)), DMA((planes,)),
            DMA((planes,)), DMA((planes, 2)), DMA((planes,)),
        ],
        compiler_params=pltpu.CompilerParams(
            collective_id=0, has_side_effects=True, vmem_limit_bytes=56 * 1024 * 1024
        ),
        cost_estimate=pl.CostEstimate(flops=7_000_000_000, bytes_accessed=8_000_000, transcendentals=3_000_000),
    )(
        latents[0], timestep, wave, norm_gain, time_weight, conv_weight, attend_weight, output_weight,
        ind, indb, e, et,
    )
    return out[None]


def fits(mesh):
    planes, dps = mesh.shape["frame"], mesh.shape["dp"]
    return planes == 4 and dps == 8


def solution(mesh):
    in_specs = (
        P("dp", "frame", None, None),
        P("dp"),
        P(),
        P("dp", None),
        P(None, ("dp", "frame"), None),
        P(("dp", "frame"), None),
        P(("dp", "frame"), None),
    )
    out_specs = P("dp", "frame", None, None)
    return jax.shard_map(fast_shards if fits(mesh) else shards, mesh=mesh, in_specs=in_specs, out_specs=out_specs, check_vma=False)
```
